32 devices in a mesh: gx: 4 (over x, core), gy: 8 (over z, y).
Axes of the slice: x: 2, y: 2, z: 4, core: 2. Of those that a mesh axis runs over, the one named last changes fastest.
Arguments:
- views: bfloat16 [384, 49, 2048], P(('gx', 'gy')), may hold values from -6 to 6
- counts: int32 [32], P(('gx', 'gy')), may hold values from 1 to 12, as said below
- partners: int32 [384, 2], P(('gx', 'gy')), may hold values from 0 to 383, as said below
- w_in: bfloat16 [2048, 512], P('gx', 'gy'), may hold values from -0.125 to 0.125
- w_mid: bfloat16 [4608, 512], P('gx', 'gy'), may hold values from -0.09375 to 0.09375
- w_out: bfloat16 [512, 2048], P('gx', 'gy'), may hold values from -0.25 to 0.25
- norm_params: bfloat16 [6144], P(('gx', 'gy')), may hold values from 0.5 to 1.5
Outputs:
- loss_value: float32 [], replicated
- views_grad: float32 [384, 49, 2048], P(('gx', 'gy'))
- w_in_grad: float32 [2048, 512], P('gx', 'gy')
- w_mid_grad: float32 [4608, 512], P('gx', 'gy')
- w_out_grad: float32 [512, 2048], P('gx', 'gy')
- norm_grad: float32 [6144], P(('gx', 'gy'))
The draws below stay inside these ranges and needn't reach their ends.
Inputs may be any that keep to these rules, and one draw needn't show every extreme that they name: A device's views fill its first counts slots; in every draw some device has all 12 slots filled and some device holds one view. Every entry names a filled slot; a filled slot never lists itself, and its partners lie mostly on other devices. Entries of empty slots are filled slots too.
All inputs are finite; a program needn't handle non-finite values.
Results may differ from the reference program's by a relative error of at most 0.017.
Values may be sent and summed in bfloat16 or wider, within the bound.
No kernel may reach another device: no remote copies, remote signals or barrier semaphores. Data moves between devices by JAX's collectives and lax.ppermute only.
A program may use at most 192 MiB of HBM per device.

```python
import jax
import jax.numpy as jnp
from jax import lax

CIN = 2048
CMID = 512
SIDE = 7
PK = 2
VCAP = 12
HW = 49
VIEWS = 384
BNP = 6144


def make_counts(key):
    folded = jax.random.fold_in(key, 11)
    first_key, second_key = jax.random.split(folded)
    device_count = VIEWS // VCAP
    drawn = jax.random.randint(first_key, (device_count,), 1, VCAP + 1)
    order = jax.random.permutation(second_key, device_count)
    drawn = drawn.at[order[0]].set(VCAP).at[order[1]].set(1)
    return drawn.astype(jnp.int32)


def draw_counts(key, part):
    return make_counts(key)


def draw_partners(key, part):
    counts = make_counts(key)
    ends = jnp.cumsum(counts).astype(jnp.int32)
    starts = ends - counts
    total_filled = ends[-1]
    slot_ids = jnp.arange(VIEWS, dtype=jnp.int32)
    slot_device = slot_ids // VCAP
    slot_place = slot_ids % VCAP
    own_rank = starts[slot_device] + jnp.minimum(slot_place, counts[slot_device] - 1)
    raw_draw = jax.random.randint(jax.random.fold_in(key, 23), (VIEWS, PK), 0, 1073741824) % (total_filled - 1)
    ranked = raw_draw + (raw_draw >= own_rank[:, None]).astype(jnp.int32)
    owner = jnp.sum((ranked[:, :, None] >= ends[None, None, :]).astype(jnp.int32), axis=2)
    return (owner * VCAP + ranked - starts[owner]).astype(jnp.int32)


def level_of(key, shape, cuts, smallest, high):
    level = 1.0
    for axis_at, parts in cuts:
        steps = jax.random.uniform(jax.random.fold_in(jax.random.fold_in(key, 6), axis_at), (parts,), jnp.float32, smallest / len(cuts), high / len(cuts))
        level = level * jnp.repeat(jnp.exp(steps), shape[axis_at] // parts).reshape((-1,) + (1,) * (len(shape) - 1 - axis_at))
    return level


def centred(rng, extent, width, reach, cuts=(), kind=jnp.bfloat16):
    values = width * jax.random.normal(rng, extent, jnp.float32)
    if cuts:
        values = values * level_of(rng, extent, cuts, -0.22, 0.18)
    return jnp.clip(values, -reach, reach).astype(kind)


def setup_inputs(seed: int = 0) -> dict:
    splits = jax.random.split(jax.random.key(seed), 8)
    views = centred(splits[0], (VIEWS, HW, CIN), 1.0, 6.0, ((0, 32),))
    counts = draw_counts(jax.random.fold_in(splits[7], 71), 0)
    partners = draw_partners(jax.random.fold_in(splits[7], 71), 0)
    w_in = centred(splits[3], (CIN, CMID), CIN ** -0.5, 0.125, ((0, 4), (1, 8)))
    w_mid = centred(splits[4], (9 * CMID, CMID), (9 * CMID) ** -0.5, 0.09375, ((0, 4), (1, 8)))
    w_out = centred(splits[5], (CMID, CIN), CMID ** -0.5, 0.25, ((0, 4), (1, 8)))
    norm_params = jnp.clip(0.5 + 1.0 * jax.random.uniform(splits[6], (BNP,), jnp.float32) ** level_of(splits[6], (BNP,), ((0, 32),), -0.2, 0.2), 0.5, 1.5).astype(jnp.bfloat16)
    return dict(views=views, counts=counts, partners=partners, w_in=w_in, w_mid=w_mid, w_out=w_out, norm_params=norm_params)


@jax.custom_vjp
def low(v):
    return lax.optimization_barrier(v.astype(jnp.bfloat16)).astype(jnp.float32)

@jax.custom_vjp
def low_back(v):
    return v

def low_keep(v):
    return (low(v), None)

def low_pass(kept, grad):
    return (grad,)

def back_keep(v):
    return (v, None)

def back_low(kept, grad):
    return (low(grad),)
low.defvjp(low_keep, low_pass)
low_back.defvjp(back_keep, back_low)

def batch_norm(hidden, gain, shift, weight):
    number = jnp.sum(weight)
    center = lax.optimization_barrier(jnp.sum(hidden * weight, axis=0)) / number
    spread = lax.optimization_barrier(jnp.sum(hidden * hidden * weight, axis=0)) / number - center * center
    return gain * ((hidden - center) * lax.rsqrt(spread + 1e-05)) + shift

def forward(views_f, w_in, w_mid, w_out, norm_values, weight, filled, partners):
    row_count = VIEWS * HW
    gain_one = norm_values[0:CMID]
    shift_one = norm_values[CMID:2 * CMID]
    gain_two = norm_values[2 * CMID:3 * CMID]
    shift_two = norm_values[3 * CMID:4 * CMID]
    gain_three = norm_values[4 * CMID:4 * CMID + CIN]
    shift_three = norm_values[4 * CMID + CIN:4 * CMID + 2 * CIN]
    flat_in = views_f.reshape(row_count, CIN)
    hidden_one = low_back(jnp.dot(flat_in, w_in, precision=lax.Precision.HIGHEST))
    active_one = low(jax.nn.silu(batch_norm(hidden_one, gain_one, shift_one, weight)))
    kernel = w_mid.reshape(3, 3, CMID, CMID)
    hidden_two = lax.conv_general_dilated(active_one.reshape(VIEWS, SIDE, SIDE, CMID), kernel, (1, 1), ((1, 1), (1, 1)), dimension_numbers=('NHWC', 'HWIO', 'NHWC'), precision=lax.Precision.HIGHEST)
    hidden_two = low_back(hidden_two.reshape(row_count, CMID))
    active_two = low(jax.nn.silu(batch_norm(hidden_two, gain_two, shift_two, weight)))
    hidden_three = low_back(jnp.dot(active_two, w_out, precision=lax.Precision.HIGHEST))
    activated = jax.nn.silu(batch_norm(hidden_three, gain_three, shift_three, weight) + flat_in)
    pooled = lax.optimization_barrier(jnp.mean(activated.reshape(VIEWS, HW, CIN), axis=1))
    embedded = low(pooled * lax.rsqrt(lax.optimization_barrier(jnp.mean(pooled * pooled, axis=1, keepdims=True)) + 1e-06))
    difference = embedded[:, None, :] - embedded[partners]
    return jnp.sum(filled[:, None, None] * difference * difference)

def reference(views, counts, partners, w_in, w_mid, w_out, norm_params):
    slot_ids = jnp.arange(VIEWS, dtype=jnp.int32)
    filled = (slot_ids % VCAP < counts[slot_ids // VCAP]).astype(jnp.float32)
    weight = jnp.repeat(filled, HW)[:, None]

    def objective_of(views_f, weight_in, weight_mid, weight_out, norm_values):
        return forward(views_f, weight_in, weight_mid, weight_out, norm_values, weight, filled, partners)
    objective, pullback = jax.vjp(objective_of, views.astype(jnp.float32), w_in.astype(jnp.float32), w_mid.astype(jnp.float32), w_out.astype(jnp.float32), norm_params.astype(jnp.float32))
    gradients = pullback(jnp.ones_like(objective))
    loss_value = objective / (PK * CIN * jnp.sum(filled))
    return (loss_value, gradients[0], gradients[1], gradients[2], gradients[3], gradients[4])
```

```python
import functools

import jax
import jax.numpy as jnp
from jax import lax
from jax.experimental import pallas as pl
from jax.experimental.pallas import tpu as pltpu
from jax.sharding import PartitionSpec as P

SIDE = 7
AX = ("gx", "gy")
BF = jnp.bfloat16
F32 = jnp.float32
NT = (((1,), (1,)), ((), ()))
NN = (((1,), (0,)), ((), ()))
TN = (((0,), (0,)), ((), ()))
VM = pl.BlockSpec(memory_space=pltpu.VMEM)
SM = pl.BlockSpec(memory_space=pltpu.SMEM)
HBM = pl.BlockSpec(memory_space=pl.ANY)
MIB = 1 << 20
GIGA = 1 << 30
LIMIT = {
    "in": 60,
    "act": 60,
    "mid": 60,
    "out": 60,
    "pool": 60,
    "pair": 60,
    "out_back": 60,
    "out_grad": 60,
    "mid_back": 60,
    "mid_grad": 60,
    "in_grad": 60,
    "views": 60,
}


def dot(left, right, dims):
    return lax.dot_general(left, right, dims, preferred_element_type=F32)


def sigmoid(value):
    return 0.5 * jnp.tanh(0.5 * value) + 0.5


def slope_of(value, sigma):
    return sigma * (1.0 + value * (1.0 - sigma))


class Net:
    def __init__(self, gx, gy):
        self.gx, self.gy, self.size = gx, gy, gx * gy
        self.core = gy
        self.across = [2 * gy * k for k in range(1, gx // 2)]
        self.side = [1]
        self.far = [2 * k for k in range(1, gy // 2)]

    def swap(self, value, mask):
        pairs = [(d, d ^ mask) for d in range(self.size)]
        return lax.ppermute(value, AX, pairs)

    def order(self):
        masks = [0] + self.far
        half = len(masks) // 2
        first, second = masks[:half], masks[half:]
        grow = lambda held, peers: held + [m ^ p for p in peers for m in held]
        first = grow(grow(first, self.across), self.side)
        second = grow(grow(second, self.side), self.across)
        chip = first + second
        return chip + [m ^ self.core for m in chip]

    def grow(self, held, peers):
        return jnp.concatenate([held] + [self.swap(held, p) for p in peers])

    def gather_far(self, own):
        held = jnp.stack([own] + [self.swap(own, m) for m in self.far])
        half = held.shape[0] // 2
        return held[:half], held[half:]

    def gather_near(self, halves):
        return self.grow(halves[0], self.across), self.grow(halves[1], self.side)

    def gather_last(self, halves):
        return jnp.concatenate([self.grow(halves[0], self.side), self.grow(halves[1], self.across)])

    def gather_core(self, chip):
        return self.grow(chip, [self.core])

    def fold(self, held, peers):
        count = len(peers) + 1
        parts = held.reshape((count, held.shape[0] // count) + held.shape[1:])
        total = parts[0].astype(F32)
        for place, mask in enumerate(peers):
            total = total + self.swap(parts[place + 1], mask).astype(F32)
        return total

    def reduce_core(self, blocks):
        chip = self.fold(blocks, [self.core]).astype(BF)
        half = chip.shape[0] // 2
        return chip[:half], chip[half:]

    def reduce_last(self, halves):
        return self.fold(halves[0], self.side).astype(BF), self.fold(halves[1], self.across).astype(BF)

    def reduce_near(self, halves):
        return self.fold(halves[0], self.across).astype(BF), self.fold(halves[1], self.side).astype(BF)

    def reduce_far(self, halves):
        return self.fold(jnp.concatenate(halves), self.far)[0]

    def spread(self, copies):
        return lax.all_to_all(copies, AX, 0, 0, tiled=True)


def tie(value, *done):
    return lax.optimization_barrier((value,) + done)[0]


class Grid:
    def __init__(self, slots, features, channels):
        self.slots, self.features, self.channels = slots, features, channels
        self.pixels = SIDE * SIDE
        self.flat = SIDE * (SIDE + 1)
        self.rows = slots * self.flat
        self.band = slots * (SIDE + 1)
        self.tall = self.rows + 2 * self.band


def call(body, outs, ins, scratch, limit, flops=0, moved=0, **extra):
    return pl.pallas_call(
        body,
        out_shape=outs,
        name=body.func.__name__,
        in_specs=ins,
        out_specs=extra.pop("out_specs", [VM] * len(outs)),
        scratch_shapes=scratch,
        compiler_params=pltpu.CompilerParams(vmem_limit_bytes=limit * MIB),
        cost_estimate=pl.CostEstimate(flops=flops, bytes_accessed=moved, transcendentals=0),
        **extra,
    )


def block_plan(net, shape):
    rows, cols, row_axis = shape
    plan = []
    for gx in range(net.gx):
        for gy in range(net.gy):
            at = (gy * rows, gx * cols) if row_axis == "gy" else (gx * rows, gy * cols)
            plan.append((at[0], at[1], rows, cols))
    return plan


def fetch(plan, slots_ref, source, target, sem):
    if plan is None:
        pltpu.make_async_copy(source, target, sem).start()
        return
    for owner, (row, col, rows, cols) in enumerate(plan):
        pltpu.make_async_copy(
            source.at[slots_ref[owner]], target.at[pl.ds(row, rows), pl.ds(col, cols)], sem
        ).start()


def arrive(target, sem):
    pltpu.make_async_copy(target, target, sem).wait()


def scatter_blocks(plan, slots_ref, source, target, sem):
    if plan is None:
        pltpu.make_async_copy(source, target, sem).start()
    else:
        for owner, (row, col, rows, cols) in enumerate(plan):
            pltpu.make_async_copy(
                source.at[pl.ds(row, rows), pl.ds(col, cols)], target.at[slots_ref[owner]], sem
            ).start()
    pltpu.make_async_copy(source, source, sem).wait()


def moments(received, number):
    total = jnp.sum(received, axis=0)
    mean = total[0:1] / number
    inverse = lax.rsqrt(total[1:2] / number - mean * mean + 1e-05)
    return mean, inverse


def copies_of(value, out_ref):
    def one(place, carry):
        out_ref[place] = value
        return carry

    lax.fori_loop(0, out_ref.shape[0], one, 0)


def typical(gs):
    reach = 1.7320508 * gs[0:1]
    total = 0.0
    for node, share in ((gs[1:2] - reach, 1 / 6), (gs[1:2], 2 / 3), (gs[1:2] + reach, 1 / 6)):
        total = total + share * node * sigmoid(node)
    return total


def pieces_of(row):
    first = row.astype(BF).astype(F32)
    second = (row - first).astype(BF).astype(F32)
    third = row - first - second
    return jnp.concatenate([first, second, third, jnp.zeros((13, row.shape[1]), F32)], axis=0).astype(BF)


def outer(left, right):
    return dot(jnp.broadcast_to(left.astype(BF), (16, left.shape[1])), pieces_of(right), TN)


def local_sum(rows_here, mine, sums, mean, inverse, gain, shift_part, gain_part):
    hats = (sums - rows_here * mean) * inverse
    return gain * inverse * (mine - rows_here * shift_part - gain_part * hats)


def row_id(rows):
    return lax.broadcasted_iota(jnp.int32, (rows, 1), 0)


def in_body(g, plan, count_ref, slots_ref, x_ref, small_ref, w_hbm, h_ref, out_ref, w_ref, st_ref, sem):
    fetch(plan, slots_ref, w_hbm, w_ref, sem)
    arrive(w_ref, sem)
    keep = (row_id(g.rows) < count_ref[0] * g.flat).astype(F32)
    step = 256
    for at in range(0, g.channels, step):
        lanes = pl.ds(at, step)
        h = dot(x_ref[...], w_ref[lanes, :], NT)
        h_ref[:, lanes] = h
        kept = h * keep
        st_ref[0:1, lanes] = jnp.sum(kept, axis=0, keepdims=True)
        st_ref[1:2, lanes] = jnp.sum(kept * h, axis=0, keepdims=True)
    st_ref[2:3] = small_ref[...]
    copies_of(st_ref[...], out_ref)


def grid_rows(g, source, place):
    view, line = place
    return source[pl.ds(view * g.flat + SIDE * line, SIDE + 1), :]


def shifted(tall, out_ref):
    out_ref[0] = pltpu.roll(tall, 1, 0).astype(BF)
    out_ref[1] = tall.astype(BF)
    out_ref[2] = pltpu.roll(tall, tall.shape[0] - 1, 0).astype(BF)


def act_body(g, h_ref, got_ref, gs_ref, a_ref, hq_ref, bn_ref, q_ref):
    total = jnp.sum(got_ref[...], axis=0)
    number = jnp.max(total[2:3, g.channels - 1 : g.channels]) * float(g.pixels)
    mean = total[0:1] / number
    inverse = lax.rsqrt(total[1:2] / number - mean * mean + 1e-05)
    bn_ref[0:1] = mean
    bn_ref[1:2] = inverse
    bn_ref[2:3] = jnp.full((1, g.channels), number, F32)
    scale, shift = gs_ref[0:1] * inverse, gs_ref[1:2]
    inside = row_id(SIDE + 1) < SIDE
    q_ref[0 : g.band] = jnp.zeros((g.band, g.channels), F32)
    q_ref[g.tall - g.band : g.tall] = jnp.zeros((g.band, g.channels), F32)
    for line in range(SIDE):
        for view in range(g.slots):
            h = grid_rows(g, h_ref, (view, line))
            at = line * g.band + view * (SIDE + 1)
            hq_ref[at : at + SIDE + 1] = h
            n = (h - mean) * scale + shift
            q_ref[g.band + at : g.band + at + SIDE + 1] = jnp.where(inside, n * sigmoid(n), 0.0)
    shifted(q_ref[...], a_ref)


def mid_body(g, plan, count_ref, slots_ref, a_ref, w_hbm, h2_ref, st_ref, out_ref, w_ref, sem):
    fetch(plan, slots_ref, w_hbm, w_ref, sem)
    c = g.channels
    row = row_id(g.rows)
    live = ((row % (SIDE + 1)) < SIDE) & ((row % g.band) < count_ref[0] * (SIDE + 1))
    keep = live.astype(F32)
    step = 256
    arrive(w_ref, sem)
    for at in range(0, c, step):
        h2 = None
        for ky in range(3):
            for kx in range(3):
                tap = 3 * ky + kx
                part = dot(
                    a_ref[kx, ky * g.band : ky * g.band + g.rows],
                    w_ref[at : at + step, tap * c : (tap + 1) * c],
                    NT,
                )
                h2 = part if h2 is None else h2 + part
        h2_ref[:, at : at + step] = h2
        kept = h2 * keep
        st_ref[0:1, at : at + step] = jnp.sum(kept, axis=0, keepdims=True)
        st_ref[1:2, at : at + step] = jnp.sum(kept * h2, axis=0, keepdims=True)
    copies_of(st_ref[...], out_ref)


def out_body(g, plan, count_ref, slots_ref, h2_ref, got_ref, bn1_ref, gs_ref, w_hbm, a2_ref, h3_ref, st_ref, out_ref, bn_ref, w_ref, p_ref, sem):
    fetch(plan, slots_ref, w_hbm, w_ref, sem)
    mean, inverse = moments(got_ref[...], bn1_ref[2:3])
    bn_ref[0:1] = mean
    bn_ref[1:2] = inverse
    scale, shift = gs_ref[0:1] * inverse, gs_ref[1:2]
    inside = row_id(SIDE + 1) < SIDE
    for view in range(g.slots):
        for line in range(SIDE):
            at = line * g.band + view * (SIDE + 1)
            n = (h2_ref[at : at + SIDE + 1] - mean) * scale + shift
            p_ref[pl.ds(view * g.flat + SIDE * line, SIDE + 1), :] = jnp.where(inside, n * sigmoid(n), 0.0)
        p_ref[pl.ds(view * g.flat + g.pixels, SIDE), :] = jnp.zeros((SIDE, g.channels), F32)
    a2_ref[...] = p_ref[...].astype(BF)
    arrive(w_ref, sem)
    keep = (row_id(g.rows) < count_ref[0] * g.flat).astype(F32)
    step = 256
    for at in range(0, g.features, step):
        lanes = slice(at, at + step)
        h = dot(a2_ref[...], w_ref[:, lanes], NN)
        h3_ref[:, lanes] = h
        kept = h * keep
        st_ref[0:1, lanes] = jnp.sum(kept, axis=0, keepdims=True)
        st_ref[1:2, lanes] = jnp.sum(kept * h, axis=0, keepdims=True)
    copies_of(st_ref[...], out_ref)


def pair_back_body(g, grad_ref, pool_ref, fac_ref, s_ref, t_ref, dp_ref, st_ref, out_ref):
    grad = grad_ref[...]
    pooled = pool_ref[...]
    factor = fac_ref[:, 0:1]
    along = jnp.sum(pooled * grad, axis=1, keepdims=True) * (1.0 / g.features)
    down = (factor * grad - pooled * (factor * factor * factor) * along) * (1.0 / g.pixels)
    dp_ref[...] = down
    st_ref[0:1] = jnp.sum(down * s_ref[...], axis=0, keepdims=True)
    st_ref[1:2] = jnp.sum(down * t_ref[...], axis=0, keepdims=True)
    copies_of(st_ref[...], out_ref)


def pool_body(g, h3_ref, x_ref, got_ref, bn1_ref, gs_ref, z_ref, pool_ref, fac_ref, s_ref, t_ref, bn_ref):
    mean, inverse = moments(got_ref[...], bn1_ref[2:3, 0:1])
    bn_ref[0:1] = mean
    bn_ref[1:2] = inverse
    real = (row_id(g.flat) < g.pixels).astype(F32)
    step = 512

    def one(view, carry):
        rows = pl.ds(pl.multiple_of(view * g.flat, 8), g.flat)
        for at in range(0, g.features, step):
            lanes = slice(at, at + step)
            hat = (h3_ref[rows, lanes] - bn_ref[0:1, lanes]) * bn_ref[1:2, lanes]
            pre = hat * gs_ref[0:1, lanes] + gs_ref[1:2, lanes] + x_ref[rows, lanes].astype(F32)
            sigma = sigmoid(pre)
            slope = slope_of(pre, sigma) * real
            out = pre * sigma * real
            pool_ref[pl.ds(view, 1), lanes] = jnp.sum(out, axis=0, keepdims=True) * (1.0 / g.pixels)
            s_ref[pl.ds(view, 1), lanes] = jnp.sum(slope, axis=0, keepdims=True)
            t_ref[pl.ds(view, 1), lanes] = jnp.sum(slope * hat, axis=0, keepdims=True)
        return carry

    lax.fori_loop(0, g.slots, one, 0)
    pooled = pool_ref[...]
    factor = lax.rsqrt(jnp.mean(pooled * pooled, axis=1, keepdims=True) + 1e-06)
    fac_ref[...] = jnp.broadcast_to(factor, fac_ref.shape)
    z_ref[...] = (pooled * factor).astype(BF)


def out_back_body(
    g, plan, count_ref, slots_ref, h3_ref, x_ref, dp_ref, got_ref, mine_ref, sums_ref, objective_ref, bn1_ref, bn3_ref, gs3_ref,
    h2_ref, bn2_ref, gs2_ref, w_hbm, dpre_ref, dh3_ref, dn2_ref, st_ref, out_ref, tot_ref, local_ref, w_ref, p_ref, c_ref, sem,
):
    fetch(plan, slots_ref, w_hbm, w_ref, sem)
    number = bn1_ref[2:3, 0:1]
    total = jnp.sum(got_ref[...], axis=0)
    tot_ref[...] = total
    c_ref[...] = total / number
    here = (count_ref[0] * g.pixels).astype(F32)
    local_ref[...] = local_sum(
        here, mine_ref[0:1], sums_ref[0:1], bn3_ref[0:1], bn3_ref[1:2], gs3_ref[0:1], c_ref[0:1], c_ref[1:2]
    )
    real = row_id(g.flat) < g.pixels
    step = 512

    def one(view, carry):
        rows = pl.ds(pl.multiple_of(view * g.flat, 8), g.flat)
        live = (real & (view < count_ref[0])).astype(F32)
        for at in range(0, g.features, step):
            lanes = slice(at, at + step)
            inverse = bn3_ref[1:2, lanes]
            gain = gs3_ref[0:1, lanes]
            hat = (h3_ref[rows, lanes] - bn3_ref[0:1, lanes]) * inverse
            pre = hat * gain + gs3_ref[1:2, lanes] + x_ref[rows, lanes].astype(F32)
            up = dp_ref[pl.ds(view, 1), lanes] * slope_of(pre, sigmoid(pre))
            dpre_ref[rows, lanes] = (up * live).astype(BF)
            down = gain * inverse * (up - c_ref[0:1, lanes] - hat * c_ref[1:2, lanes])
            dh3_ref[rows, lanes] = (down * live).astype(BF)
        return carry

    lax.fori_loop(0, g.slots, one, 0)
    arrive(w_ref, sem)
    p_ref[...] = dot(dh3_ref[...], w_ref[...], NT)
    mean, inverse = bn2_ref[0:1], bn2_ref[1:2]
    gain, shift = gs2_ref[0:1], gs2_ref[1:2]
    inside = row_id(SIDE + 1) < SIDE
    first = jnp.zeros((SIDE + 1, g.channels), F32)
    second = jnp.zeros((SIDE + 1, g.channels), F32)
    for line in range(SIDE):
        for view in range(g.slots):
            at = line * g.band + view * (SIDE + 1)
            hat = (h2_ref[at : at + SIDE + 1] - mean) * inverse
            n = hat * gain + shift
            up = jnp.where(inside, grid_rows(g, p_ref, (view, line)) * slope_of(n, sigmoid(n)), 0.0)
            dn2_ref[at : at + SIDE + 1] = up
            first = first + up
            second = second + up * hat
    st_ref[0:1] = jnp.sum(first, axis=0, keepdims=True)
    st_ref[1:2] = jnp.sum(second, axis=0, keepdims=True)
    st_ref[2:3] = objective_ref[...]
    copies_of(st_ref[...], out_ref)


def out_grad_body(g, plan, slots_ref, a2_ref, dh3_ref, gs2_ref, local_ref, out_hbm, w_ref, sem):
    base = typical(gs2_ref[...])
    step = 512
    for at in range(0, g.features, step):
        lanes = slice(at, at + step)
        grad = dot(a2_ref[...], dh3_ref[:, lanes], TN) - outer(base, local_ref[:, lanes])
        w_ref[:, lanes] = grad.astype(BF)
    scatter_blocks(plan, slots_ref, w_ref, out_hbm, sem)


def norm_back(up, hat, live, gain, inverse, shift_part, gain_part):
    return gain * inverse * (up - live * (shift_part + hat * gain_part))


def mid_back_body(
    g, plan, count_ref, slots_ref, dn2_ref, got_ref, mine_ref, sums_ref, bn1_ref, bn2_ref, gs2_ref, h2_ref, hq_ref, gs1_ref, w_hbm,
    dh2_ref, dn1_ref, out_ref, tot_ref, local_ref, w_ref, q_ref, d_ref, st_ref, sem,
):
    fetch(plan, slots_ref, w_hbm, w_ref, sem)
    number = bn1_ref[2:3, 0:1]
    total = jnp.sum(got_ref[...], axis=0)
    tot_ref[...] = total
    shift_part, gain_part = total[0:1] / number, total[1:2] / number
    here = (count_ref[0] * g.pixels).astype(F32)
    local_ref[...] = local_sum(
        here, mine_ref[0:1], sums_ref[0:1], bn2_ref[0:1], bn2_ref[1:2], gs2_ref[0:1], shift_part, gain_part
    )
    rows = row_id(g.rows)
    live = (((rows % (SIDE + 1)) < SIDE) & ((rows % g.band) < count_ref[0] * (SIDE + 1))).astype(F32)
    hat = (h2_ref[...] - bn2_ref[0:1]) * bn2_ref[1:2]
    down = norm_back(dn2_ref[...], hat, live, gs2_ref[0:1], bn2_ref[1:2], shift_part, gain_part)
    dh2_ref[...] = down.astype(BF)
    q_ref[0 : g.band] = jnp.zeros((g.band, g.channels), F32)
    q_ref[g.tall - g.band : g.tall] = jnp.zeros((g.band, g.channels), F32)
    q_ref[g.band : g.tall - g.band] = down
    shifted(q_ref[...], d_ref)
    arrive(w_ref, sem)
    c = g.channels
    inside = (rows % (SIDE + 1)) < SIDE
    step = 256
    for at in range(0, c, step):
        lanes = slice(at, at + step)
        da1 = None
        for ky in range(3):
            for kx in range(3):
                tap = 3 * ky + kx
                part = dot(
                    d_ref[2 - kx, (2 - ky) * g.band : (2 - ky) * g.band + g.rows],
                    w_ref[:, tap * c + at : tap * c + at + step],
                    NN,
                )
                da1 = part if da1 is None else da1 + part
        hat1 = (hq_ref[:, lanes] - bn1_ref[0:1, lanes]) * bn1_ref[1:2, lanes]
        n = hat1 * gs1_ref[0:1, lanes] + gs1_ref[1:2, lanes]
        up = jnp.where(inside, da1 * slope_of(n, sigmoid(n)), 0.0)
        dn1_ref[:, lanes] = up
        st_ref[0:1, lanes] = jnp.sum(up, axis=0, keepdims=True)
        st_ref[1:2, lanes] = jnp.sum(up * hat1, axis=0, keepdims=True)
    copies_of(st_ref[...], out_ref)


def mid_grad_body(g, plan, slots_ref, dh2_ref, a_ref, gs1_ref, local_ref, out_hbm, w_ref, base_ref, sem):
    c = g.channels
    shared = jnp.broadcast_to(typical(gs1_ref[...]).astype(BF), (16, c))
    base_ref[...] = dot(pieces_of(local_ref[...]), shared, TN)
    for ky in range(3):
        for kx in range(3):
            tap = 3 * ky + kx
            part = dot(dh2_ref[...], a_ref[kx, ky * g.band : ky * g.band + g.rows], TN)
            w_ref[:, tap * c : (tap + 1) * c] = (part - base_ref[...]).astype(BF)
    scatter_blocks(plan, slots_ref, w_ref, out_hbm, sem)


def in_grad_body(
    g, plan, count_ref, slots_ref, dn1_ref, got_ref, bn1_ref, gs1_ref, hq_ref, x_ref, dh1_ref, tot_ref, out_hbm, w_ref, p_ref, sem
):
    number = bn1_ref[2:3, 0:1]
    total = jnp.sum(got_ref[...], axis=0)
    tot_ref[...] = total
    shift_part, gain_part = total[0:1] / number, total[1:2] / number
    mean, inverse = bn1_ref[0:1], bn1_ref[1:2]
    for view in range(g.slots):
        live = ((row_id(SIDE + 1) < SIDE) & (view < count_ref[0])).astype(F32)
        for line in range(SIDE):
            at = line * g.band + view * (SIDE + 1)
            hat = (hq_ref[at : at + SIDE + 1] - mean) * inverse
            down = norm_back(dn1_ref[at : at + SIDE + 1], hat, live, gs1_ref[0:1], inverse, shift_part, gain_part)
            p_ref[pl.ds(view * g.flat + SIDE * line, SIDE + 1), :] = down
        p_ref[pl.ds(view * g.flat + g.pixels, SIDE), :] = jnp.zeros((SIDE, g.channels), F32)
    dh1_ref[...] = p_ref[...].astype(BF)
    step = 512
    for at in range(0, g.features, step):
        lanes = slice(at, at + step)
        w_ref[:, lanes] = dot(dh1_ref[...], x_ref[:, lanes], TN).astype(BF)
    scatter_blocks(plan, slots_ref, w_ref, out_hbm, sem)


def views_grad_body(g, plan, slots_ref, dh1_ref, dpre_ref, w_hbm, out_ref, w_ref, sem):
    @pl.when(pl.program_id(0) == 0)
    def _():
        fetch(plan, slots_ref, w_hbm, w_ref, sem)
        arrive(w_ref, sem)

    step = out_ref.shape[2]
    lanes = pl.ds(pl.multiple_of(pl.program_id(0) * step, step), step)
    total = dot(dh1_ref[...], w_ref[:, lanes], NN) + dpre_ref[...].astype(F32)
    for view in range(g.slots):
        out_ref[view] = total[view * g.flat : view * g.flat + g.pixels]


def per_device(views, counts, partners, w_in, w_mid, w_out, norm_params):
    slot_count, pixels, features = views.shape
    pair_count = partners.shape[1]
    net = Net(lax.axis_size("gx"), lax.axis_size("gy"))
    size = net.size
    channels = w_in.shape[1] * net.gy
    g = Grid(slot_count, features, channels)
    me = lax.axis_index("gx") * net.gy + lax.axis_index("gy")
    order = net.order()
    place = [order.index(mask) for mask in range(size)]
    slots = jnp.asarray(place, jnp.int32)[me ^ jnp.arange(size, dtype=jnp.int32)]
    sources = me ^ jnp.asarray(order, jnp.int32)

    shards = {"in": (w_in.T, "gy"), "mid": (w_mid.T, "gy"), "out": (w_out, "gx")}
    plans, whole_of = {}, {}
    for name, (shard, row_axis) in shards.items():
        rows, cols = shard.shape
        aligned = rows % 16 == 0 and cols % 128 == 0
        plans[name] = block_plan(net, (rows, cols, row_axis)) if aligned else None
        whole_of[name] = (rows * (net.gy if row_axis == "gy" else net.gx), cols * (net.gx if row_axis == "gy" else net.gy))

    def pick(places, blocks):
        chooser = (places[:, None] == jnp.arange(size, dtype=jnp.int32)[None, :]).astype(BF)
        return jnp.dot(chooser, blocks.reshape(size, -1), preferred_element_type=F32).astype(BF).reshape(blocks.shape)

    def whole(name, held):
        if plans[name] is not None:
            return held
        shard, row_axis = shards[name]
        held = pick(slots, held).reshape((net.gx, net.gy) + shard.shape)
        return held.transpose((1, 2, 0, 3) if row_axis == "gy" else (0, 2, 1, 3)).reshape(whole_of[name])

    def in_order(name, grads):
        if plans[name] is not None:
            return grads
        shard, row_axis = shards[name]
        rows, cols = shard.shape
        if row_axis == "gy":
            grads = grads.reshape(net.gy, rows, net.gx, cols).transpose(2, 0, 1, 3)
        else:
            grads = grads.reshape(net.gx, rows, net.gy, cols).transpose(0, 2, 1, 3)
        return pick(sources, grads.reshape(size, rows, cols))

    def grad_shape(name):
        if plans[name] is None:
            return jax.ShapeDtypeStruct(whole_of[name], BF)
        return jax.ShapeDtypeStruct((size,) + shards[name][0].shape, BF)

    held_in = net.gather_far(shards["in"][0])
    held_mid = net.gather_far(tie(shards["mid"][0], held_in))
    held_in = net.gather_near(held_in)
    held_out = net.gather_far(tie(shards["out"][0], held_mid, held_in))
    held_in = net.gather_last(held_in)
    held_mid = net.gather_near(tie(held_mid, held_in))
    full_in = whole("in", net.gather_core(held_in))

    sem = pltpu.SemaphoreType.DMA(())
    f32 = lambda *shape: jax.ShapeDtypeStruct(shape, F32)
    b16 = lambda *shape: jax.ShapeDtypeStruct(shape, BF)
    weight = lambda name: pltpu.VMEM(whole_of[name], BF)

    x = jnp.pad(views, ((0, 0), (0, g.flat - pixels), (0, 0))).reshape(g.rows, features)
    share = norm_params.shape[0]
    listed = slot_count * pair_count
    small = jnp.concatenate(
        [
            norm_params.astype(F32),
            partners.reshape(-1).astype(F32),
            jnp.zeros((channels - 1 - share - listed,), F32),
            counts.astype(F32),
        ]
    )[None]

    h1, copies = call(
        functools.partial(in_body, g, plans["in"]),
        [f32(g.rows, channels), f32(size, 3, channels)],
        [SM, SM, VM, VM, HBM],
        [weight("in"), pltpu.VMEM((3, channels), F32), sem],
        LIMIT["in"],
        flops=4 * GIGA,
    )(counts, slots, x, small, full_in)
    got = net.spread(copies)
    held_mid = net.gather_last(tie(held_mid, h1))
    full_mid = whole("mid", net.gather_core(held_mid))
    held_out = net.gather_near(tie(held_out, held_mid, got))

    norm_values = got[:, 2, :share].reshape(-1)
    gs1 = norm_values[0 : 2 * channels].reshape(2, channels)
    gs2 = norm_values[2 * channels : 4 * channels].reshape(2, channels)
    gs3 = norm_values[4 * channels :].reshape(2, features)

    a1, h1q, bn1 = call(
        functools.partial(act_body, g),
        [b16(3, g.tall, channels), f32(g.rows, channels), f32(3, channels)],
        [VM, VM, VM],
        [pltpu.VMEM((g.tall, channels), F32)],
        LIMIT["act"],
        flops=20 * GIGA,
    )(h1, got, gs1)
    h2, sums2, copies = call(
        functools.partial(mid_body, g, plans["mid"]),
        [f32(g.rows, channels), f32(2, channels), f32(size, 2, channels)],
        [SM, SM, VM, HBM],
        [weight("mid"), sem],
        LIMIT["mid"],
        flops=9 * GIGA,
    )(counts, slots, a1, full_mid)
    targets = got[:, 2, share : share + listed].reshape(size * slot_count, pair_count).astype(jnp.int32)
    occupied = got[:, 2, channels - 1]
    got = net.spread(copies)
    held_out = net.gather_last(tie(held_out, h2))
    full_out = whole("out", net.gather_core(held_out))

    a2, h3, sums3, copies, bn2 = call(
        functools.partial(out_body, g, plans["out"]),
        [b16(g.rows, channels), f32(g.rows, features), f32(2, features), f32(size, 2, features), f32(2, channels)],
        [SM, SM, VM, VM, VM, VM, HBM],
        [weight("out"), pltpu.VMEM((g.rows, channels), F32), sem],
        LIMIT["out"],
        flops=8 * GIGA,
    )(counts, slots, h2, got, bn1, gs2, full_out)

    got = net.spread(copies)
    view_ids = jnp.arange(size * slot_count, dtype=jnp.int32)
    filled = ((view_ids % slot_count).astype(F32) < jnp.repeat(occupied, slot_count)).astype(F32)
    chosen = [(targets[:, k : k + 1] == view_ids[None, :]).astype(F32) * filled[:, None] for k in range(pair_count)]
    pairs = sum(chosen)
    links = pairs + pairs.T
    degree = jnp.sum(links, axis=1, keepdims=True)
    z, pooled, factor, slope_sum, slope_hat, bn3 = call(
        functools.partial(pool_body, g),
        [b16(slot_count, features), f32(slot_count, features), f32(slot_count, 128)]
        + [f32(slot_count, features)] * 2
        + [f32(2, features)],
        [VM] * 5,
        [],
        LIMIT["pool"],
        flops=8 * GIGA,
    )(h3, x, got, bn1, gs3)

    width = features // size
    pieces = lax.all_to_all(z.reshape(slot_count, size, width).transpose(1, 0, 2), AX, 0, 0, tiled=True)
    held = pieces.reshape(size * slot_count, width)
    held_f = held.astype(F32)
    grad_embed = 2.0 * (degree * held_f - jnp.dot(links.astype(BF), held, preferred_element_type=F32))
    objective = 0.0
    for one in chosen:
        gap = filled[:, None] * held_f - jnp.dot(one.astype(BF), held, preferred_element_type=F32)
        objective = objective + jnp.sum(gap * gap)
    objective = jnp.full((1, channels), objective, F32)
    grad_embed = lax.all_to_all(grad_embed.reshape(size, slot_count, width), AX, 0, 0, tiled=True)
    grad_embed = grad_embed.transpose(1, 0, 2).reshape(slot_count, features)

    grad_pooled, mine3, copies = call(
        functools.partial(pair_back_body, g),
        [f32(slot_count, features), f32(2, features), f32(size, 2, features)],
        [VM] * 5,
        [],
        LIMIT["pair"],
        flops=2 * GIGA,
    )(grad_embed, pooled, factor, slope_sum, slope_hat)
    got = net.spread(copies)
    dpre, dh3, dn2, mine2, copies, total3, local3 = call(
        functools.partial(out_back_body, g, plans["out"]),
        [
            b16(g.rows, features),
            b16(g.rows, features),
            f32(g.rows, channels),
            f32(3, channels),
            f32(size, 3, channels),
            f32(2, features),
            f32(1, features),
        ],
        [SM, SM] + [VM] * 13 + [HBM],
        [weight("out"), pltpu.VMEM((g.rows, channels), F32), pltpu.VMEM((2, features), F32), sem],
        LIMIT["out_back"],
        flops=10 * GIGA,
    )(counts, slots, h3, x, grad_pooled, got, mine3, sums3, objective, bn1, bn3, gs3, h2, bn2, gs2, full_out)

    got = net.spread(copies)
    out_blocks = call(
        functools.partial(out_grad_body, g, plans["out"]),
        [grad_shape("out")],
        [SM, VM, VM, VM, VM],
        [weight("out"), sem],
        LIMIT["out_grad"],
        flops=4 * GIGA,
        out_specs=[HBM],
    )(slots, a2, dh3, gs2, local3)[0]
    sum_out = net.reduce_core(in_order("out", out_blocks))

    dh2, dn1, copies, total2, local2 = call(
        functools.partial(mid_back_body, g, plans["mid"]),
        [b16(g.rows, channels), f32(g.rows, channels), f32(size, 2, channels), f32(3, channels), f32(1, channels)],
        [SM, SM] + [VM] * 10 + [HBM],
        [
            weight("mid"),
            pltpu.VMEM((g.tall, channels), F32),
            pltpu.VMEM((3, g.tall, channels), BF),
            pltpu.VMEM((2, channels), F32),
            sem,
        ],
        LIMIT["mid_back"],
        flops=12 * GIGA,
    )(counts, slots, dn2, got, mine2, sums2, bn1, bn2, gs2, h2, h1q, gs1, full_mid)
    got = net.spread(copies)
    sum_out = net.reduce_last(sum_out)
    mid_blocks = call(
        functools.partial(mid_grad_body, g, plans["mid"]),
        [grad_shape("mid")],
        [SM, VM, VM, VM, VM],
        [weight("mid"), pltpu.VMEM((channels, channels), F32), sem],
        LIMIT["mid_grad"],
        flops=6 * GIGA,
        out_specs=[HBM],
    )(slots, tie(dh2, sum_out), a1, gs1, local2)[0]
    sum_mid = net.reduce_core(in_order("mid", mid_blocks))
    sum_out = net.reduce_near(sum_out)

    dh1, total1, in_blocks = call(
        functools.partial(in_grad_body, g, plans["in"]),
        [b16(g.rows, channels), f32(2, channels), grad_shape("in")],
        [SM, SM] + [VM] * 6,
        [weight("in"), pltpu.VMEM((g.rows, channels), F32), sem],
        LIMIT["in_grad"],
        flops=6 * GIGA,
        out_specs=[VM, VM, HBM],
    )(counts, slots, dn1, tie(got, sum_mid), bn1, gs1, h1q, x)
    sum_in = net.reduce_core(in_order("in", in_blocks))

    step = 512
    whole_rows = lambda cols: pl.BlockSpec((g.rows, cols), lambda i: (0, 0))
    views_grad = pl.pallas_call(
        functools.partial(views_grad_body, g, plans["in"]),
        grid=(features // step,),
        out_shape=f32(slot_count, pixels, features),
        in_specs=[SM, whole_rows(channels), pl.BlockSpec((g.rows, step), lambda i: (0, i)), HBM],
        out_specs=pl.BlockSpec((slot_count, pixels, step), lambda i: (0, 0, i)),
        scratch_shapes=[weight("in"), sem],
        compiler_params=pltpu.CompilerParams(vmem_limit_bytes=LIMIT["views"] * MIB),
        cost_estimate=pl.CostEstimate(flops=6 * GIGA, bytes_accessed=0, transcendentals=0),
        name="views_grad_body",
    )(slots, dh1, dpre, full_in)

    own_out = net.reduce_far(sum_out)
    sum_mid = net.reduce_last(sum_mid)
    sum_in = net.reduce_last(sum_in)
    sum_mid = net.reduce_near(sum_mid)
    sum_in = net.reduce_near(sum_in)
    own_mid = net.reduce_far(sum_mid).T
    own_in = net.reduce_far(sum_in).T

    loss_value = total2[2, 0] / (pair_count * features * jnp.sum(occupied))
    norm_full = jnp.concatenate([total1[1], total1[0], total2[1], total2[0], total3[1], total3[0]])
    norm_grad = lax.dynamic_slice_in_dim(norm_full, me * share, share)
    return (loss_value, views_grad, own_in, own_mid, own_out, norm_grad)


def solution(mesh):
    weights = P("gx", "gy")
    in_specs = (P(AX, None, None), P(AX), P(AX, None), weights, weights, weights, P(AX))
    out_specs = (P(), P(AX, None, None), weights, weights, weights, P(AX))
    return jax.shard_map(
        per_device, mesh=mesh, in_specs=in_specs, out_specs=out_specs, check_vma=False
    )
```

```python
import functools

import jax
import jax.numpy as jnp
from jax import lax
from jax.experimental import pallas as pl
from jax.experimental.pallas import tpu as pltpu
from jax.sharding import PartitionSpec as P

SIDE = 7
AX = ("gx", "gy")
BF = jnp.bfloat16
F32 = jnp.float32
NT = (((1,), (1,)), ((), ()))
NN = (((1,), (0,)), ((), ()))
TN = (((0,), (0,)), ((), ()))
VM = pl.BlockSpec(memory_space=pltpu.VMEM)
SM = pl.BlockSpec(memory_space=pltpu.SMEM)
HBM = pl.BlockSpec(memory_space=pl.ANY)
MIB = 1 << 20
COST = pl.CostEstimate(flops=60 << 30, bytes_accessed=0, transcendentals=0)
LIMIT = 60


def dot(left, right, dims):
    return lax.dot_general(left, right, dims, preferred_element_type=F32)


def sigmoid(value):
    return 0.5 * jnp.tanh(0.5 * value) + 0.5


def slope_of(value, sigma):
    return sigma * (1.0 + value * (1.0 - sigma))


def tie(value, *done):
    return lax.optimization_barrier((value,) + done)[0]


class Net:
    def __init__(self, gx, gy):
        self.gx, self.gy, self.size = gx, gy, gx * gy
        self.core = gy
        self.across = [2 * gy * k for k in range(1, gx // 2)]
        self.side = 1
        self.far = [2 * k for k in range(1, gy // 2)]
        line = [0] + self.far
        self.half = half = len(line) // 2
        self.pieces = {"own": line}
        for p in self.across:
            self.pieces[f"x{p}"] = [m ^ p for m in line]
        self.pieces["y"] = [m ^ self.side for m in line]
        for p in self.across:
            self.pieces[f"xyA{p}"] = [m ^ self.side ^ p for m in line[:half]]
            self.pieces[f"xyB{p}"] = [m ^ self.side ^ p for m in line[half:]]

    def order(self):
        chip = [m for masks in self.pieces.values() for m in masks]
        return chip + [m ^ self.core for m in chip]

    def swap(self, value, mask):
        pairs = [(d, d ^ mask) for d in range(self.size)]
        return lax.ppermute(value, AX, pairs)

    def gather_far(self, own):
        return {"own": jnp.stack([own] + [self.swap(own, m) for m in self.far])}

    def gather_near(self, held):
        more = {f"x{p}": self.swap(held["own"], p) for p in self.across}
        more["y"] = self.swap(held["own"], self.side)
        return more

    def gather_last(self, near):
        more = {}
        for p in self.across:
            more[f"xyA{p}"] = self.swap(near[f"x{p}"][: self.half], self.side)
            more[f"xyB{p}"] = self.swap(near["y"][self.half :], p)
        return more

    def gather_core(self, held):
        chip = [held[name] for name in self.pieces]
        return chip + [self.swap(piece, self.core) for piece in chip]

    def reduce_core(self, keep, away, *done):
        got = self.swap(away, self.core)
        keep = tie(keep, *done)
        pieces = {}
        start = 0
        for name, masks in self.pieces.items():
            span = slice(start, start + len(masks))
            pieces[name] = add(keep[span], got[span])
            start = span.stop
        return pieces

    def reduce_last(self, pieces):
        half = self.half
        out = {"own": pieces["own"]}
        for p in self.across:
            held = pieces[f"x{p}"]
            out[f"x{p}"] = jnp.concatenate([add(held[:half], self.swap(pieces[f"xyA{p}"], self.side)), held[half:]])
        back = [self.swap(pieces[f"xyB{p}"], p) for p in self.across]
        out["y"] = jnp.concatenate([pieces["y"][:half], add(pieces["y"][half:], *back)])
        return out

    def reduce_near(self, pieces):
        back = [self.swap(pieces[f"x{p}"], p) for p in self.across] + [self.swap(pieces["y"], self.side)]
        return [add(pieces["own"][i], *[one[i] for one in back]) for i in range(len(self.far) + 1)]

    def reduce_far(self, line):
        total = line[0].astype(F32)
        for block, mask in zip(line[1:], self.far):
            total = total + self.swap(block, mask).astype(F32)
        return total

    def spread(self, copies):
        return lax.all_to_all(copies, AX, 0, 0, tiled=True)


def add(*terms):
    return sum(term.astype(F32) for term in terms).astype(BF)


class Grid:
    def __init__(self, slots, features, channels):
        self.slots, self.features, self.channels = slots, features, channels
        self.pixels = SIDE * SIDE
        self.flat = SIDE * (SIDE + 1)
        self.rows = slots * self.flat
        self.band = slots * (SIDE + 1)
        self.tall = self.rows + 2 * self.band
        self.chunk = 2 * self.flat
        self.chunks = slots // 2


class Blocks:
    def __init__(self, net, shape, tall_axis):
        self.net, self.shape, self.tall_axis = net, shape, tall_axis
        self.rows, self.cols = shape
        down, beside = (net.gy, net.gx) if tall_axis == "gy" else (net.gx, net.gy)
        self.whole = (self.rows * down, self.cols * beside)
        self.beside = beside
        self.aligned = self.rows % 16 == 0 and self.cols % 128 == 0
        self.order = net.order()

    def spot(self, owner):
        ox, oy = owner // self.net.gy, owner % self.net.gy
        down, beside = (oy, ox) if self.tall_axis == "gy" else (ox, oy)
        if isinstance(owner, int):
            return pl.ds(down * self.rows, self.rows), pl.ds(beside * self.cols, self.cols), beside
        row = pl.multiple_of(down * self.rows, self.rows)
        col = pl.multiple_of(beside * self.cols, self.cols)
        return pl.ds(row, self.rows), pl.ds(col, self.cols), beside

    def fetch(self, me, sources, target, sems):
        if not self.aligned:
            pltpu.make_async_copy(sources[0], target, sems.at[0]).start()
            return
        masks = iter(self.order)
        for source in sources:
            for place in range(source.shape[0]):
                rows, cols, beside = self.spot(me ^ next(masks))
                pltpu.make_async_copy(source.at[place], target.at[rows, cols], sems.at[beside]).start()

    def arrive(self, target, sems, beside):
        if not self.aligned:
            if beside == 0:
                pltpu.make_async_copy(target, target, sems.at[0]).wait()
            return
        part = target.at[:, pl.ds(beside * self.cols, self.cols)]
        pltpu.make_async_copy(part, part, sems.at[beside]).wait()

    def arrive_to(self, target, sems, done, col):
        while done < self.beside and done * self.cols < col:
            self.arrive(target, sems, done)
            done += 1
        return done

    def send(self, slots_ref, source, targets, sem, beside):
        if not self.aligned:
            if beside == self.beside - 1:
                pltpu.make_async_copy(source, targets[0], sem).start()
            return
        net = self.net
        half = net.size // 2
        for other in range(net.gy if self.tall_axis == "gy" else net.gx):
            owner = beside * net.gy + other if self.tall_axis == "gy" else other * net.gy + beside
            rows, cols, _ = self.spot(owner)
            slot = slots_ref[owner]

            @pl.when(slot < half)
            def _():
                pltpu.make_async_copy(source.at[rows, cols], targets[0].at[slot], sem).start()

            @pl.when(slot >= half)
            def _():
                pltpu.make_async_copy(source.at[rows, cols], targets[1].at[slot - half], sem).start()

    def send_to(self, slots_ref, source, targets, sem, done, col):
        while done < self.beside and (done + 1) * self.cols <= col:
            self.send(slots_ref, source, targets, sem, done)
            done += 1
        return done


def call(body, outs, ins, scratch, out_specs=None, limit=LIMIT):
    return pl.pallas_call(
        body,
        out_shape=outs,
        name=body.func.__name__,
        in_specs=ins,
        out_specs=[VM] * len(outs) if out_specs is None else out_specs,
        scratch_shapes=scratch,
        compiler_params=pltpu.CompilerParams(vmem_limit_bytes=limit * MIB),
        cost_estimate=COST,
    )


def begin(source, target, sem):
    pltpu.make_async_copy(source, target, sem).start()


def end(target, sem):
    pltpu.make_async_copy(target, target, sem).wait()


def moments(received, number):
    total = jnp.sum(received, axis=0)
    mean = total[0:1] / number
    inverse = lax.rsqrt(total[1:2] / number - mean * mean + 1e-05)
    return mean, inverse


def copies_of(value, out_ref):
    def one(place, carry):
        out_ref[place] = value
        return carry

    lax.fori_loop(0, out_ref.shape[0], one, 0)


def typical(gs):
    reach = 1.7320508 * gs[0:1]
    total = 0.0
    for node, share in ((gs[1:2] - reach, 1 / 6), (gs[1:2], 2 / 3), (gs[1:2] + reach, 1 / 6)):
        total = total + share * node * sigmoid(node)
    return total


def pieces_of(row):
    first = row.astype(BF).astype(F32)
    second = (row - first).astype(BF).astype(F32)
    third = row - first - second
    return jnp.concatenate([first, second, third, jnp.zeros((13, row.shape[1]), F32)], axis=0).astype(BF)


def outer(left, right):
    return dot(jnp.broadcast_to(left.astype(BF), (16, left.shape[1])), pieces_of(right), TN)


def local_sum(rows_here, mine, sums, mean, inverse, gain, shift_part, gain_part):
    hats = (sums - rows_here * mean) * inverse
    return gain * inverse * (mine - rows_here * shift_part - gain_part * hats)


def norm_back(up, hat, live, gain, inverse, shift_part, gain_part):
    return gain * inverse * (up - live * (shift_part + hat * gain_part))


def row_id(rows):
    return lax.broadcasted_iota(jnp.int32, (rows, 1), 0)


def column_sums(total_ref, lanes, keep, chunk, base=None):
    first, second = 0.0, 0.0
    for at in range(0, total_ref.shape[0], chunk):
        value = total_ref[at : at + chunk, lanes]
        if base is not None:
            value = value - base
        kept = value * keep[at : at + chunk]
        first = first + jnp.sum(kept, axis=0, keepdims=True)
        second = second + jnp.sum(kept * value, axis=0, keepdims=True)
    return first, second


def in_body(g, blocks, count, info_ref, x_ref, small_ref, *refs):
    sources = refs[:count]
    h_ref, out_ref, w_ref, st_ref, wsem = refs[count:]
    blocks.fetch(info_ref[1], sources, w_ref, wsem)
    keep = (row_id(g.rows) < info_ref[0] * g.flat).astype(F32)
    step = 256
    blocks.arrive_to(w_ref, wsem, 0, g.features)
    for at in range(0, g.channels, step):
        lanes = slice(at, at + step)
        h_ref[:, lanes] = dot(x_ref[...], w_ref[lanes, :], NT)
        st_ref[0:1, lanes], st_ref[1:2, lanes] = column_sums(h_ref, lanes, keep, g.chunk)
    st_ref[2:3] = small_ref[...]
    copies_of(st_ref[...], out_ref)


def flat_rows(g, source, line, lanes):
    return jnp.concatenate(
        [source[pl.ds(view * g.flat + SIDE * line, SIDE + 1), lanes] for view in range(g.slots)], axis=0
    )


def to_flat(g, band, target, line, lanes):
    for view in range(g.slots):
        target[pl.ds(view * g.flat + SIDE * line, SIDE + 1), lanes] = band[view * (SIDE + 1) : (view + 1) * (SIDE + 1)]


def clear_padding(g, target):
    for view in range(g.slots):
        target[pl.ds(view * g.flat + g.pixels, SIDE), :] = jnp.zeros((SIDE, target.shape[1]), F32)


def band_mask(g):
    return (row_id(g.band) % (SIDE + 1)) < SIDE


def shift_rows(g, tall_ref, out_ref):
    for kx in range(3):
        for at in range(0, g.tall, g.band):
            start, stop = at + kx - 1, at + kx - 1 + g.band
            if start < 0 or stop > g.tall:
                rows = pltpu.roll(tall_ref[at : at + g.band], (1 - kx) % g.band, 0)
            else:
                rows = tall_ref[start:stop]
            out_ref[kx, at : at + g.band] = rows.astype(BF)


def mid_body(g, blocks, count, info_ref, h_ref, got_ref, gs_ref, *refs):
    sources = refs[:count]
    a_hbm, hat_ref, h2_ref, st_ref, out_ref, bn_ref, a_ref, w_ref, q_ref, wsem, osem = refs[count:]
    blocks.fetch(info_ref[1], sources, w_ref, wsem)
    c = g.channels
    total = jnp.sum(got_ref[...], axis=0)
    number = jnp.max(total[2:3, c - 1 : c]) * float(g.pixels)
    mean = total[0:1] / number
    inverse = lax.rsqrt(total[1:2] / number - mean * mean + 1e-05)
    bn_ref[0:1] = mean
    bn_ref[1:2] = inverse
    bn_ref[2:3] = jnp.full((1, c), number, F32)
    inside = band_mask(g)
    q_ref[0 : g.band] = jnp.zeros((g.band, c), F32)
    q_ref[g.tall - g.band : g.tall] = jnp.zeros((g.band, c), F32)
    step = 256
    for line in range(SIDE):
        at = line * g.band
        for lane in range(0, c, step):
            lanes = slice(lane, lane + step)
            hat = (flat_rows(g, h_ref, line, lanes) - mean[:, lanes]) * inverse[:, lanes]
            hat_ref[at : at + g.band, lanes] = hat.astype(BF)
            n = hat * gs_ref[0:1, lanes] + gs_ref[1:2, lanes]
            q_ref[g.band + at : 2 * g.band + at, lanes] = jnp.where(inside, n * sigmoid(n), 0.0)
    shift_rows(g, q_ref, a_ref)
    begin(a_ref, a_hbm, osem)
    row = row_id(g.rows)
    live = ((row % (SIDE + 1)) < SIDE) & ((row % g.band) < info_ref[0] * (SIDE + 1))
    keep = live.astype(F32)
    done = 0
    for at in range(0, c, step):
        h2 = None
        for ky in range(3):
            for kx in range(3):
                tap = 3 * ky + kx
                done = blocks.arrive_to(w_ref, wsem, done, c * 9)
                part = dot(
                    a_ref[kx, ky * g.band : ky * g.band + g.rows],
                    w_ref[at : at + step, tap * c : (tap + 1) * c],
                    NT,
                )
                h2 = part if h2 is None else h2 + part
        lanes = slice(at, at + step)
        h2_ref[:, lanes] = h2
        st_ref[0:1, lanes], st_ref[1:2, lanes] = column_sums(h2_ref, lanes, keep, g.band)
    copies_of(st_ref[...], out_ref)
    end(a_ref, osem)


def out_body(g, blocks, count, info_ref, h2_ref, got_ref, bn1_ref, gs_ref, *refs):
    sources = refs[:count]
    a2_ref, h3_hbm, st_ref, out_ref, bn_ref, hat_ref, w_ref, p_ref, t_ref, h3_ref, mo_ref, wsem, osem = refs[count:]
    blocks.fetch(info_ref[1], sources, w_ref, wsem)
    mean, inverse = moments(got_ref[...], bn1_ref[2:3])
    bn_ref[0:1] = mean
    bn_ref[1:2] = inverse
    inside = band_mask(g)
    c = g.channels
    step = 256
    clear_padding(g, p_ref)
    for line in range(SIDE):
        at = line * g.band
        for lane in range(0, c, step):
            lanes = slice(lane, lane + step)
            hat = (h2_ref[at : at + g.band, lanes] - mean[:, lanes]) * inverse[:, lanes]
            hat_ref[at : at + g.band, lanes] = hat.astype(BF)
            n = hat * gs_ref[0:1, lanes] + gs_ref[1:2, lanes]
            to_flat(g, jnp.where(inside, n * sigmoid(n), 0.0), p_ref, line, lanes)
    p_ref[g.pixels : g.pixels + 1] = typical(gs_ref[...])
    for at in range(0, g.rows, g.chunk):
        a2_ref[at : at + g.chunk] = p_ref[at : at + g.chunk].astype(BF)
    row = row_id(g.rows)
    keep = (((row % g.flat) < g.pixels) & (row < info_ref[0] * g.flat)).astype(F32)
    here = (info_ref[0] * g.pixels).astype(F32)
    done = 0
    for at in range(0, g.features, step):
        lanes = slice(at, at + step)
        done = blocks.arrive_to(w_ref, wsem, done, at + step)
        t_ref[...] = dot(a2_ref[...], w_ref[:, lanes], NN)
        base = t_ref[g.pixels : g.pixels + 1]
        for top in range(0, g.rows, g.chunk):
            h3_ref[top : top + g.chunk, lanes] = (t_ref[top : top + g.chunk] - base).astype(BF)
        begin(h3_ref.at[:, pl.ds(at, step)], h3_hbm.at[:, pl.ds(at, step)], osem)
        total, square = column_sums(t_ref, slice(0, step), keep, g.chunk, base)
        st_ref[0:1, lanes] = total
        mo_ref[0:1, lanes] = total / here
        mo_ref[1:2, lanes] = square - total * total / here
    copies_of(mo_ref[...].astype(BF), out_ref)
    end(h3_ref, osem)


def pool_body(
    g, h3_hbm, x_hbm, got_ref, counts_ref, bn1_ref, gs_ref, z_ref, pool_ref, fac_ref, s_ref, t_ref, bn_ref, slope_hbm, hat_hbm,
    h3_ref, x_ref, slope_ref, hat_ref, insem, osem,
):
    for chunk in range(g.chunks):
        rows = pl.ds(chunk * g.chunk, g.chunk)
        begin(h3_hbm.at[rows], h3_ref.at[rows], insem.at[chunk, 0])
        begin(x_hbm.at[rows], x_ref.at[rows], insem.at[chunk, 1])
    number = bn1_ref[2:3, 0:1]
    rows_of = counts_ref[...] * float(g.pixels)
    means = got_ref[:, 0, :].astype(F32)
    mean = jnp.sum(rows_of * means, axis=0, keepdims=True) / number
    apart = means - mean
    square = got_ref[:, 1, :].astype(F32) + rows_of * apart * apart
    bn_ref[0:1] = mean
    bn_ref[1:2] = lax.rsqrt(jnp.sum(square, axis=0, keepdims=True) / number + 1e-05)
    real = ((row_id(g.chunk) % g.flat) < g.pixels).astype(F32)
    step = 256

    def one(chunk, carry):
        rows = pl.ds(pl.multiple_of(chunk * g.chunk, 16), g.chunk)
        end(h3_ref.at[rows], insem.at[chunk, 0])
        end(x_ref.at[rows], insem.at[chunk, 1])
        for at in range(0, g.features, step):
            lanes = slice(at, at + step)
            hat = (h3_ref[rows, lanes].astype(F32) - bn_ref[0:1, lanes]) * bn_ref[1:2, lanes]
            pre = hat * gs_ref[0:1, lanes] + gs_ref[1:2, lanes] + x_ref[rows, lanes].astype(F32)
            sigma = sigmoid(pre)
            slope = slope_of(pre, sigma) * real
            out = pre * sigma * real
            hat_ref[rows, lanes] = hat.astype(BF)
            slope_ref[rows, lanes] = slope.astype(BF)
            for table, value in ((pool_ref, out * (1.0 / g.pixels)), (s_ref, slope), (t_ref, slope * hat)):
                for one_of in range(2):
                    part = value[one_of * g.flat : (one_of + 1) * g.flat]
                    table[pl.ds(2 * chunk + one_of, 1), lanes] = jnp.sum(part, axis=0, keepdims=True)
        begin(slope_ref.at[rows], slope_hbm.at[rows], osem.at[0])
        begin(hat_ref.at[rows], hat_hbm.at[rows], osem.at[1])
        return carry

    lax.fori_loop(0, g.chunks, one, 0)
    pooled = pool_ref[...]
    factor = lax.rsqrt(jnp.mean(pooled * pooled, axis=1, keepdims=True) + 1e-06)
    fac_ref[...] = jnp.broadcast_to(factor, fac_ref.shape)
    z_ref[...] = (pooled * factor).astype(BF)
    end(slope_ref, osem.at[0])
    end(hat_ref, osem.at[1])


def pair_back_body(g, grad_ref, pool_ref, fac_ref, s_ref, t_ref, dp_ref, st_ref, out_ref):
    grad = grad_ref[...]
    pooled = pool_ref[...]
    factor = fac_ref[:, 0:1]
    along = jnp.sum(pooled * grad, axis=1, keepdims=True) * (1.0 / g.features)
    down = (factor * grad - pooled * (factor * factor * factor) * along) * (1.0 / g.pixels)
    dp_ref[...] = down
    st_ref[0:1] = jnp.sum(down * s_ref[...], axis=0, keepdims=True)
    st_ref[1:2] = jnp.sum(down * t_ref[...], axis=0, keepdims=True)
    copies_of(st_ref[...].astype(out_ref.dtype), out_ref)


def out_back_body(
    g, blocks, count, info_ref, slope_hbm, hat_hbm, dp_ref, got_ref, mine_ref, sums_ref, objective_ref, bn1_ref, bn3_ref, gs3_ref,
    hat2_hbm, gs2_ref, *refs,
):
    sources = refs[:count]
    dh3_hbm, dn2_ref, st_ref, out_ref, tot_ref, local_ref = refs[count : count + 6]
    slope_ref, hat_ref, dh3_ref, hat2_ref, w_ref, p_ref, c_ref, insem, hsem, wsem, osem = refs[count + 6 :]
    for chunk in range(g.chunks):
        rows = pl.ds(chunk * g.chunk, g.chunk)
        begin(slope_hbm.at[rows], slope_ref.at[rows], insem.at[chunk, 0])
        begin(hat_hbm.at[rows], hat_ref.at[rows], insem.at[chunk, 1])
    blocks.fetch(info_ref[1], sources, w_ref, wsem)
    begin(hat2_hbm, hat2_ref, hsem)
    number = bn1_ref[2:3, 0:1]
    total = jnp.sum(got_ref[...].astype(F32), axis=0)
    tot_ref[...] = total
    c_ref[0:2] = total / number
    c_ref[2:3] = gs3_ref[0:1] * bn3_ref[1:2]
    here = (info_ref[0] * g.pixels).astype(F32)
    local_ref[...] = local_sum(
        here, mine_ref[0:1], sums_ref[0:1], bn3_ref[0:1], bn3_ref[1:2], gs3_ref[0:1], c_ref[0:1], c_ref[1:2]
    )
    row = row_id(g.flat)
    step = 512

    def one(chunk, carry):
        rows = pl.ds(pl.multiple_of(chunk * g.chunk, 16), g.chunk)
        end(slope_ref.at[rows], insem.at[chunk, 0])
        end(hat_ref.at[rows], insem.at[chunk, 1])
        for at in range(0, g.features, step):
            lanes = slice(at, at + step)
            slope, hat = slope_ref[rows, lanes].astype(F32), hat_ref[rows, lanes].astype(F32)
            parts = []
            for one_of in range(2):
                view = 2 * chunk + one_of
                span = slice(one_of * g.flat, (one_of + 1) * g.flat)
                live = ((row < g.pixels) & (view < info_ref[0])).astype(F32)
                up = dp_ref[pl.ds(view, 1), lanes] * slope[span]
                parts.append(c_ref[2:3, lanes] * (up - live * (c_ref[0:1, lanes] + hat[span] * c_ref[1:2, lanes])))
            dh3_ref[rows, lanes] = jnp.concatenate(parts, axis=0).astype(BF)
        begin(dh3_ref.at[rows], dh3_hbm.at[rows], osem.at[0])
        return carry

    lax.fori_loop(0, g.chunks, one, 0)
    blocks.arrive_to(w_ref, wsem, 0, g.features)
    p_ref[...] = dot(dh3_ref[...], w_ref[...], NT)
    end(hat2_ref, hsem)
    inside = band_mask(g)
    step = 256
    for lane in range(0, g.channels, step):
        lanes = slice(lane, lane + step)
        first, second = 0.0, 0.0
        for line in range(SIDE):
            at = line * g.band
            hat = hat2_ref[at : at + g.band, lanes].astype(F32)
            n = hat * gs2_ref[0:1, lanes] + gs2_ref[1:2, lanes]
            up = jnp.where(inside, flat_rows(g, p_ref, line, lanes) * slope_of(n, sigmoid(n)), 0.0)
            dn2_ref[at : at + g.band, lanes] = up.astype(BF)
            first = first + jnp.sum(up, axis=0, keepdims=True)
            second = second + jnp.sum(up * hat, axis=0, keepdims=True)
        st_ref[0:1, lanes] = first
        st_ref[1:2, lanes] = second
    st_ref[2:3] = objective_ref[...]
    copies_of(st_ref[...], out_ref)
    end(dh3_ref, osem.at[0])


def out_grad_body(g, blocks, slots_ref, a2_hbm, dh3_hbm, gs2_ref, local_ref, *refs):
    targets, (a2_ref, dh3_ref, w_ref, insem, dsem, osem) = refs[:-6], refs[-6:]
    begin(a2_hbm, a2_ref, insem)
    step = 512
    for place, at in enumerate(range(0, g.features, step)):
        begin(dh3_hbm.at[:, pl.ds(at, step)], dh3_ref.at[:, pl.ds(at, step)], dsem.at[place])
    base = typical(gs2_ref[...])
    end(a2_ref, insem)
    done = 0
    for place, at in enumerate(range(0, g.features, step)):
        lanes = slice(at, at + step)
        end(dh3_ref.at[:, pl.ds(at, step)], dsem.at[place])
        grad = dot(a2_ref[...], dh3_ref[:, lanes], TN) - outer(base, local_ref[:, lanes])
        w_ref[:, lanes] = grad.astype(BF)
        done = blocks.send_to(slots_ref, w_ref, targets, osem, done, at + step)
    end(w_ref, osem)


def mid_back_body(
    g, blocks, count, info_ref, dn2_ref, got_ref, mine_ref, sums_ref, bn1_ref, bn2_ref, gs2_ref, hat2_ref, hat1_ref, gs1_ref, *refs,
):
    sources = refs[:count]
    dh2_ref, dn1_ref, out_ref, tot_ref, local_ref, w_ref, q_ref, d_ref, t_ref, st_ref, wsem = refs[count:]
    blocks.fetch(info_ref[1], sources, w_ref, wsem)
    number = bn1_ref[2:3, 0:1]
    total = jnp.sum(got_ref[...], axis=0)
    tot_ref[...] = total
    shift_part, gain_part = total[0:1] / number, total[1:2] / number
    here = (info_ref[0] * g.pixels).astype(F32)
    local_ref[...] = local_sum(
        here, mine_ref[0:1], sums_ref[0:1], bn2_ref[0:1], bn2_ref[1:2], gs2_ref[0:1], shift_part, gain_part
    )
    c = g.channels
    inside = band_mask(g)
    live = (inside & (row_id(g.band) < info_ref[0] * (SIDE + 1))).astype(F32)
    q_ref[0 : g.band] = jnp.zeros((g.band, c), F32)
    q_ref[g.tall - g.band : g.tall] = jnp.zeros((g.band, c), F32)
    step = 256
    for line in range(SIDE):
        at = line * g.band
        for lane in range(0, c, step):
            lanes = slice(lane, lane + step)
            hat = hat2_ref[at : at + g.band, lanes].astype(F32)
            down = norm_back(
                dn2_ref[at : at + g.band, lanes].astype(F32),
                hat,
                live,
                gs2_ref[0:1, lanes],
                bn2_ref[1:2, lanes],
                shift_part[:, lanes],
                gain_part[:, lanes],
            )
            dh2_ref[at : at + g.band, lanes] = down.astype(BF)
            q_ref[g.band + at : 2 * g.band + at, lanes] = down
    shift_rows(g, q_ref, d_ref)
    blocks.arrive_to(w_ref, wsem, 0, 9 * c)
    for lane in range(0, c, step):
        lanes = slice(lane, lane + step)
        da1 = None
        for ky in range(3):
            for kx in range(3):
                tap = 3 * ky + kx
                part = dot(
                    d_ref[2 - kx, (2 - ky) * g.band : (2 - ky) * g.band + g.rows],
                    w_ref[:, tap * c + lane : tap * c + lane + step],
                    NN,
                )
                da1 = part if da1 is None else da1 + part
        t_ref[...] = da1
        first, second = 0.0, 0.0
        for line in range(SIDE):
            at = line * g.band
            hat = hat1_ref[at : at + g.band, lanes].astype(F32)
            n = hat * gs1_ref[0:1, lanes] + gs1_ref[1:2, lanes]
            up = jnp.where(inside, t_ref[at : at + g.band] * slope_of(n, sigmoid(n)), 0.0)
            dn1_ref[at : at + g.band, lanes] = up.astype(BF)
            first = first + jnp.sum(up, axis=0, keepdims=True)
            second = second + jnp.sum(up * hat, axis=0, keepdims=True)
        st_ref[0:1, lanes] = first
        st_ref[1:2, lanes] = second
    copies_of(st_ref[...], out_ref)


def mid_grad_body(g, blocks, slots_ref, dh2_hbm, a_hbm, gs1_ref, local_ref, *refs):
    targets, (dh2_ref, a_ref, w_ref, base_ref, insem, asem, osem) = refs[:-7], refs[-7:]
    begin(dh2_hbm, dh2_ref, insem)
    for kx in range(3):
        begin(a_hbm.at[kx], a_ref.at[kx], asem.at[kx])
    c = g.channels
    shared = jnp.broadcast_to(typical(gs1_ref[...]).astype(BF), (16, c))
    base_ref[...] = dot(pieces_of(local_ref[...]), shared, TN)
    end(dh2_ref, insem)
    done = 0
    for ky in range(3):
        for kx in range(3):
            tap = 3 * ky + kx
            if ky == 0:
                end(a_ref.at[kx], asem.at[kx])
            part = dot(dh2_ref[...], a_ref[kx, ky * g.band : ky * g.band + g.rows], TN)
            w_ref[:, tap * c : (tap + 1) * c] = (part - base_ref[...]).astype(BF)
            done = blocks.send_to(slots_ref, w_ref, targets, osem, done, (tap + 1) * c)
    end(w_ref, osem)


def in_back_body(g, info_ref, dn1_ref, got_ref, bn1_ref, gs1_ref, hat1_ref, dh1_ref, tot_ref, p_ref):
    number = bn1_ref[2:3, 0:1]
    total = jnp.sum(got_ref[...], axis=0)
    tot_ref[...] = total
    shift_part, gain_part = total[0:1] / number, total[1:2] / number
    live = (band_mask(g) & (row_id(g.band) < info_ref[0] * (SIDE + 1))).astype(F32)
    clear_padding(g, p_ref)
    step = 256
    for line in range(SIDE):
        at = line * g.band
        for lane in range(0, g.channels, step):
            lanes = slice(lane, lane + step)
            down = norm_back(
                dn1_ref[at : at + g.band, lanes].astype(F32),
                hat1_ref[at : at + g.band, lanes].astype(F32),
                live,
                gs1_ref[0:1, lanes],
                bn1_ref[1:2, lanes],
                shift_part[:, lanes],
                gain_part[:, lanes],
            )
            to_flat(g, down, p_ref, line, lanes)
    for at in range(0, g.rows, g.chunk):
        dh1_ref[at : at + g.chunk] = p_ref[at : at + g.chunk].astype(BF)


def in_grad_body(g, blocks, slots_ref, dh1_ref, x_hbm, *refs):
    targets, (x_ref, w_ref, xsem, gsem) = refs[:-4], refs[-4:]
    step = 512
    for place, at in enumerate(range(0, g.features, step)):
        begin(x_hbm.at[:, pl.ds(at, step)], x_ref.at[:, pl.ds(at, step)], xsem.at[place])
    done = 0
    for place, at in enumerate(range(0, g.features, step)):
        lanes = slice(at, at + step)
        end(x_ref.at[:, pl.ds(at, step)], xsem.at[place])
        w_ref[:, lanes] = dot(dh1_ref[...], x_ref[:, lanes], TN).astype(BF)
        done = blocks.send_to(slots_ref, w_ref, targets, gsem, done, at + step)
    end(w_ref, gsem)


def views_grad_body(g, blocks, count, info_ref, dh1_ref, slope_ref, dp_ref, *refs):
    sources = refs[:count]
    out_ref, w_ref, wsem = refs[count:]
    step = out_ref.shape[2]
    turn = pl.program_id(0)

    @pl.when(turn == 0)
    def _():
        blocks.fetch(info_ref[1], sources, w_ref, wsem)

    for one_of in range(g.features // step):

        @pl.when(turn == one_of)
        def _():
            done = -(-one_of * step // blocks.cols) if blocks.aligned else one_of
            blocks.arrive_to(w_ref, wsem, done, (one_of + 1) * step)

    lanes = pl.ds(pl.multiple_of(turn * step, step), step)
    total = dot(dh1_ref[...], w_ref[:, lanes], NN)
    slope = slope_ref[...].astype(F32)
    for view in range(g.slots):
        rows = slice(view * g.flat, view * g.flat + g.pixels)
        out_ref[view] = total[rows] + dp_ref[view : view + 1] * slope[rows]


def per_device(views, counts, partners, w_in, w_mid, w_out, norm_params):
    slot_count, pixels, features = views.shape
    pair_count = partners.shape[1]
    net = Net(lax.axis_size("gx"), lax.axis_size("gy"))
    size = net.size
    channels = w_in.shape[1] * net.gy
    g = Grid(slot_count, features, channels)
    me = lax.axis_index("gx") * net.gy + lax.axis_index("gy")
    order = net.order()
    place = [order.index(mask) for mask in range(size)]
    slots = jnp.asarray(place, jnp.int32)[me ^ jnp.arange(size, dtype=jnp.int32)]
    sources = me ^ jnp.asarray(order, jnp.int32)
    info = jnp.stack([counts[0], me.astype(jnp.int32)])

    shards = {"in": w_in.T, "mid": w_mid.T, "out": w_out}
    blocks = {
        name: Blocks(net, shard.shape, "gx" if name == "out" else "gy") for name, shard in shards.items()
    }

    def pick(places, table):
        chooser = (places[:, None] == jnp.arange(size, dtype=jnp.int32)[None, :]).astype(BF)
        return jnp.dot(chooser, table.reshape(size, -1), preferred_element_type=F32).astype(BF).reshape(table.shape)

    def whole(name, held):
        pieces = net.gather_core(held)
        plan = blocks[name]
        if plan.aligned:
            return pieces
        table = pick(slots, jnp.concatenate(pieces)).reshape((net.gx, net.gy) + plan.shape)
        return [table.transpose((1, 2, 0, 3) if plan.tall_axis == "gy" else (0, 2, 1, 3)).reshape(plan.whole)]

    def grad_shapes(name):
        plan = blocks[name]
        if plan.aligned:
            return [jax.ShapeDtypeStruct((size // 2,) + plan.shape, BF)] * 2
        return [jax.ShapeDtypeStruct(plan.whole, BF)]

    def reduce_core(name, grads, *done):
        plan = blocks[name]
        if not plan.aligned:
            rows, cols = plan.shape
            if plan.tall_axis == "gy":
                table = grads[0].reshape(net.gy, rows, net.gx, cols).transpose(2, 0, 1, 3)
            else:
                table = grads[0].reshape(net.gx, rows, net.gy, cols).transpose(0, 2, 1, 3)
            table = pick(sources, table.reshape(size, rows, cols))
            grads = [table[: size // 2], table[size // 2 :]]
        return net.reduce_core(*grads, *done)

    sem = pltpu.SemaphoreType.DMA
    f32 = lambda *shape: jax.ShapeDtypeStruct(shape, F32)
    b16 = lambda *shape: jax.ShapeDtypeStruct(shape, BF)
    v32 = lambda *shape: pltpu.VMEM(shape, F32)
    v16 = lambda *shape: pltpu.VMEM(shape, BF)
    weight = lambda name: pltpu.VMEM(blocks[name].whole, BF)
    arrivals = lambda name: sem((blocks[name].beside,))

    held_in = net.gather_far(shards["in"])
    x = jnp.pad(views, ((0, 0), (0, g.flat - pixels), (0, 0))).reshape(g.rows, features)
    held_mid = net.gather_far(tie(shards["mid"], held_in))
    held_in |= net.gather_near(held_in)
    held_in = tie(held_in, x, slots, info)
    held_out = net.gather_far(tie(shards["out"], held_mid))
    held_in |= net.gather_last(held_in)
    held_mid |= net.gather_near(tie(held_mid, held_in))
    held_out = tie(held_out, held_in)
    full_in = whole("in", held_in)
    share = norm_params.shape[0]
    listed = slot_count * pair_count
    small = jnp.concatenate(
        [
            norm_params.astype(F32),
            partners.reshape(-1).astype(F32),
            jnp.zeros((channels - 1 - share - listed,), F32),
            counts.astype(F32),
        ]
    )[None]

    pieces = len(full_in)
    h1, copies = call(
        functools.partial(in_body, g, blocks["in"], pieces),
        [f32(g.rows, channels), f32(size, 3, channels)],
        [SM, VM, VM] + [HBM] * pieces,
        [weight("in"), v32(3, channels), arrivals("in")],
        limit=24,
    )(info, x, small, *full_in)
    got = net.spread(tie(copies, held_mid))
    held_mid |= net.gather_last(tie(held_mid, h1))
    full_mid = whole("mid", held_mid)

    norm_values = got[:, 2, :share].reshape(-1)
    gs1 = norm_values[0 : 2 * channels].reshape(2, channels)
    gs2 = norm_values[2 * channels : 4 * channels].reshape(2, channels)
    gs3 = norm_values[4 * channels :].reshape(2, features)

    held_out |= net.gather_near(tie(held_out, held_mid, gs1))
    pieces = len(full_mid)
    a1, hat1, h2, sums2, copies, bn1 = call(
        functools.partial(mid_body, g, blocks["mid"], pieces),
        [
            b16(3, g.tall, channels),
            b16(g.rows, channels),
            f32(g.rows, channels),
            f32(2, channels),
            f32(size, 2, channels),
            f32(3, channels),
        ],
        [SM, VM, VM, VM] + [HBM] * pieces,
        [v16(3, g.tall, channels), weight("mid"), v32(g.tall, channels), arrivals("mid"), sem(())],
        out_specs=[HBM, VM, VM, VM, VM, VM],
    )(info, h1, got, gs1, *full_mid)
    targets = got[:, 2, share : share + listed].reshape(size * slot_count, pair_count).astype(jnp.int32)
    occupied = got[:, 2, channels - 1]
    got = net.spread(copies)
    held_out = tie(held_out, h2)
    held_out |= net.gather_last(held_out)
    full_out = whole("out", held_out)

    pieces = len(full_out)
    a2, h3, sums3, copies, bn2, hat2 = call(
        functools.partial(out_body, g, blocks["out"], pieces),
        [
            b16(g.rows, channels),
            b16(g.rows, features),
            f32(1, features),
            b16(size, 2, features),
            f32(2, channels),
            b16(g.rows, channels),
        ],
        [SM, VM, VM, VM, VM] + [HBM] * pieces,
        [
            weight("out"),
            v32(g.rows, channels),
            v32(g.rows, 256),
            v16(g.rows, features),
            v32(2, features),
            arrivals("out"),
            sem(()),
        ],
        out_specs=[VM, HBM, VM, VM, VM, VM],
    )(info, h2, got, bn1, gs2, *full_out)

    got = net.spread(copies)
    view_ids = jnp.arange(size * slot_count, dtype=jnp.int32)
    filled = ((view_ids % slot_count).astype(F32) < jnp.repeat(occupied, slot_count)).astype(F32)
    chosen = [(targets[:, k : k + 1] == view_ids[None, :]).astype(F32) * filled[:, None] for k in range(pair_count)]
    pairs = sum(chosen)
    links = pairs + pairs.T
    degree = jnp.sum(links, axis=1, keepdims=True)
    per_view = f32(slot_count, features)
    z, pooled, factor, slope_sum, slope_hat, bn3, slope, hat = call(
        functools.partial(pool_body, g),
        [b16(slot_count, features), per_view, f32(slot_count, 128), per_view, per_view, f32(2, features)]
        + [b16(g.rows, features)] * 2,
        [HBM, HBM] + [VM] * 4,
        [
            v16(g.rows, features),
            v16(g.rows, features),
            v16(g.rows, features),
            v16(g.rows, features),
            sem((g.chunks, 2)),
            sem((2,)),
        ],
        out_specs=[VM] * 6 + [HBM] * 2,
    )(h3, x, got, occupied[:, None], bn1, gs3)

    width = features // size
    embeds = lax.all_to_all(z.reshape(slot_count, size, width).transpose(1, 0, 2), AX, 0, 0, tiled=True)
    embeds = embeds.reshape(size * slot_count, width)
    embeds_f = embeds.astype(F32)
    grad_embed = 2.0 * (degree * embeds_f - jnp.dot(links.astype(BF), embeds, preferred_element_type=F32))
    objective = 0.0
    for one in chosen:
        gap = filled[:, None] * embeds_f - jnp.dot(one.astype(BF), embeds, preferred_element_type=F32)
        objective = objective + jnp.sum(gap * gap)
    objective = jnp.full((1, channels), objective, F32)
    grad_embed = lax.all_to_all(grad_embed.reshape(size, slot_count, width), AX, 0, 0, tiled=True)
    grad_embed = grad_embed.transpose(1, 0, 2).reshape(slot_count, features)

    grad_pooled, mine3, copies = call(
        functools.partial(pair_back_body, g),
        [per_view, f32(2, features), b16(size, 2, features)],
        [VM] * 5,
        [],
    )(grad_embed, pooled, factor, slope_sum, slope_hat)
    got = net.spread(copies)
    pieces = len(full_out)
    dh3, dn2, mine2, copies, total3, local3 = call(
        functools.partial(out_back_body, g, blocks["out"], pieces),
        [
            b16(g.rows, features),
            b16(g.rows, channels),
            f32(3, channels),
            f32(size, 3, channels),
            f32(2, features),
            f32(1, features),
        ],
        [SM, HBM, HBM] + [VM] * 8 + [HBM, VM] + [HBM] * pieces,
        [
            v16(g.rows, features),
            v16(g.rows, features),
            v16(g.rows, features),
            v16(g.rows, channels),
            weight("out"),
            v32(g.rows, channels),
            v32(3, features),
            sem((g.chunks, 2)),
            sem(()),
            arrivals("out"),
            sem((2,)),
        ],
        out_specs=[HBM, VM, VM, VM, VM, VM],
    )(info, slope, hat, grad_pooled, got, mine3, sums3, objective, bn1, bn3, gs3, hat2, gs2, *full_out)

    got = net.spread(copies)
    grads = call(
        functools.partial(out_grad_body, g, blocks["out"]),
        grad_shapes("out"),
        [SM, HBM, HBM, VM, VM],
        [v16(g.rows, channels), v16(g.rows, features), weight("out"), sem(()), sem((features // 512,)), sem(())],
        out_specs=[HBM] * len(grad_shapes("out")),
    )(slots, a2, dh3, gs2, local3)
    sum_out = reduce_core("out", grads)

    pieces = len(full_mid)
    dh2, dn1, copies, total2, local2 = call(
        functools.partial(mid_back_body, g, blocks["mid"], pieces),
        [b16(g.rows, channels), b16(g.rows, channels), f32(size, 2, channels), f32(3, channels), f32(1, channels)],
        [SM] + [VM] * 10 + [HBM] * pieces,
        [
            weight("mid"),
            v32(g.tall, channels),
            v16(3, g.tall, channels),
            v32(g.rows, 256),
            v32(2, channels),
            arrivals("mid"),
        ],
    )(info, dn2, tie(got, *grads), mine2, sums2, bn1, bn2, gs2, hat2, hat1, gs1, *full_mid)
    got = net.spread(copies)
    grads = call(
        functools.partial(mid_grad_body, g, blocks["mid"]),
        grad_shapes("mid"),
        [SM, HBM, HBM, VM, VM],
        [
            v16(g.rows, channels),
            v16(3, g.tall, channels),
            weight("mid"),
            v32(channels, channels),
            sem(()),
            sem((3,)),
            sem(()),
        ],
        out_specs=[HBM] * len(grad_shapes("mid")),
    )(slots, dh2, a1, gs1, local2)
    sum_mid = reduce_core("mid", grads)

    dh1, total1 = call(
        functools.partial(in_back_body, g),
        [b16(g.rows, channels), f32(2, channels)],
        [SM] + [VM] * 5,
        [v32(g.rows, channels)],
    )(info, dn1, tie(got, *grads), bn1, gs1, hat1)
    grads = call(
        functools.partial(in_grad_body, g, blocks["in"]),
        grad_shapes("in"),
        [SM, VM, HBM],
        [v16(g.rows, features), weight("in"), sem((features // 512,)), sem(())],
        out_specs=[HBM] * len(grad_shapes("in")),
    )(slots, tie(dh1, sum_mid), x)
    sum_mid = net.reduce_last(sum_mid)
    sum_out = net.reduce_last(tie(sum_out, *grads))
    sum_in = reduce_core("in", grads, sum_mid)

    step = 512
    pieces = len(full_in)
    whole_rows = lambda cols: pl.BlockSpec((g.rows, cols), lambda i: (0, 0))
    views_grad = pl.pallas_call(
        functools.partial(views_grad_body, g, blocks["in"], pieces),
        grid=(features // step,),
        out_shape=f32(slot_count, pixels, features),
        in_specs=[
            SM,
            whole_rows(channels),
            pl.BlockSpec((g.rows, step), lambda i: (0, i)),
            pl.BlockSpec((slot_count, step), lambda i: (0, i)),
        ]
        + [HBM] * pieces,
        out_specs=pl.BlockSpec((slot_count, pixels, step), lambda i: (0, 0, i)),
        scratch_shapes=[weight("in"), arrivals("in")],
        compiler_params=pltpu.CompilerParams(vmem_limit_bytes=LIMIT * MIB),
        cost_estimate=COST,
        name="views_grad_body",
    )(info, tie(dh1, sum_in), slope, grad_pooled, *full_in)

    sum_in = net.reduce_last(sum_in)
    own_out = net.reduce_far(net.reduce_near(sum_out))
    sum_mid = tie(net.reduce_near(sum_mid), views_grad)
    sum_in = net.reduce_near(tie(sum_in, views_grad))
    own_mid = net.reduce_far(sum_mid).T
    own_in = net.reduce_far(sum_in).T

    loss_value = total2[2, 0] / (pair_count * features * jnp.sum(occupied))
    norm_full = jnp.concatenate([total1[1], total1[0], total2[1], total2[0], total3[1], total3[0]])
    norm_grad = lax.dynamic_slice_in_dim(norm_full, me * share, share)
    return (loss_value, views_grad, own_in, own_mid, own_out, norm_grad)


def solution(mesh):
    weights = P("gx", "gy")
    in_specs = (P(AX, None, None), P(AX), P(AX, None), weights, weights, weights, P(AX))
    out_specs = (P(), P(AX, None, None), weights, weights, weights, P(AX))
    return jax.shard_map(
        per_device, mesh=mesh, in_specs=in_specs, out_specs=out_specs, check_vma=False
    )
```

```python
import functools

import jax
import jax.numpy as jnp
from jax import lax
from jax.experimental import pallas as pl
from jax.experimental.pallas import tpu as pltpu
from jax.sharding import PartitionSpec as P

SIDE = 7
AX = ("gx", "gy")
BF = jnp.bfloat16
F32 = jnp.float32
NT = (((1,), (1,)), ((), ()))
NN = (((1,), (0,)), ((), ()))
TN = (((0,), (0,)), ((), ()))
VM = pl.BlockSpec(memory_space=pltpu.VMEM)
SM = pl.BlockSpec(memory_space=pltpu.SMEM)
HBM = pl.BlockSpec(memory_space=pl.ANY)
MIB = 1 << 20
COST = pl.CostEstimate(flops=60 << 30, bytes_accessed=0, transcendentals=0)
LIMIT = 60


def dot(left, right, dims):
    return lax.dot_general(left, right, dims, preferred_element_type=F32)


def sigmoid(value):
    return 0.5 * jnp.tanh(0.5 * value) + 0.5


def slope_of(value, sigma):
    return sigma * (1.0 + value * (1.0 - sigma))


def tie(value, *done):
    return lax.optimization_barrier((value,) + done)[0]


class Net:
    def __init__(self, gx, gy):
        self.gx, self.gy, self.size = gx, gy, gx * gy
        self.core = gy
        self.across = [2 * gy * k for k in range(1, gx // 2)]
        self.side = 1
        self.far = [2 * k for k in range(1, gy // 2)]
        line = [0] + self.far
        self.half = half = len(line) // 2
        self.pieces = {"own": line}
        for p in self.across:
            self.pieces[f"x{p}"] = [m ^ p for m in line]
        self.pieces["y"] = [m ^ self.side for m in line]
        for p in self.across:
            self.pieces[f"xyA{p}"] = [m ^ self.side ^ p for m in line[:half]]
            self.pieces[f"xyB{p}"] = [m ^ self.side ^ p for m in line[half:]]

    def order(self):
        chip = [m for masks in self.pieces.values() for m in masks]
        return chip + [m ^ self.core for m in chip]

    def swap(self, value, mask):
        pairs = [(d, d ^ mask) for d in range(self.size)]
        return lax.ppermute(value, AX, pairs)

    def gather_far(self, own):
        return {"own": jnp.stack([own] + [self.swap(own, m) for m in self.far])}

    def gather_near(self, held):
        more = {f"x{p}": self.swap(held["own"], p) for p in self.across}
        more["y"] = self.swap(held["own"], self.side)
        return more

    def gather_last(self, near):
        more = {}
        for p in self.across:
            more[f"xyA{p}"] = self.swap(near[f"x{p}"][: self.half], self.side)
            more[f"xyB{p}"] = self.swap(near["y"][self.half :], p)
        return more

    def gather_core(self, held):
        chip = [held[name] for name in self.pieces]
        return chip + [self.swap(piece, self.core) for piece in chip]

    def reduce_core(self, keep, away, *done):
        got = self.swap(away, self.core)
        keep = tie(keep, *done)
        pieces = {}
        start = 0
        for name, masks in self.pieces.items():
            span = slice(start, start + len(masks))
            pieces[name] = add(keep[span], got[span])
            start = span.stop
        return pieces

    def reduce_last(self, pieces):
        half = self.half
        out = {"own": pieces["own"]}
        for p in self.across:
            held = pieces[f"x{p}"]
            out[f"x{p}"] = jnp.concatenate([add(held[:half], self.swap(pieces[f"xyA{p}"], self.side)), held[half:]])
        back = [self.swap(pieces[f"xyB{p}"], p) for p in self.across]
        out["y"] = jnp.concatenate([pieces["y"][:half], add(pieces["y"][half:], *back)])
        return out

    def reduce_near(self, pieces):
        back = [self.swap(pieces[f"x{p}"], p) for p in self.across] + [self.swap(pieces["y"], self.side)]
        return [add(pieces["own"][i], *[one[i] for one in back]) for i in range(len(self.far) + 1)]

    def reduce_far(self, line):
        total = line[0].astype(F32)
        for block, mask in zip(line[1:], self.far):
            total = total + self.swap(block, mask).astype(F32)
        return total

    def spread(self, copies):
        return lax.all_to_all(copies, AX, 0, 0, tiled=True)


def add(*terms):
    return sum(term.astype(F32) for term in terms).astype(BF)


class Grid:
    def __init__(self, slots, features, channels):
        self.slots, self.features, self.channels = slots, features, channels
        self.pixels = SIDE * SIDE
        self.flat = SIDE * (SIDE + 1)
        self.rows = slots * self.flat
        self.band = slots * (SIDE + 1)
        self.tall = self.rows + 2 * self.band
        self.chunk = 2 * self.flat
        self.chunks = slots // 2


class Blocks:
    def __init__(self, net, shape, tall_axis):
        self.net, self.shape, self.tall_axis = net, shape, tall_axis
        self.rows, self.cols = shape
        down, beside = (net.gy, net.gx) if tall_axis == "gy" else (net.gx, net.gy)
        self.whole = (self.rows * down, self.cols * beside)
        self.beside = beside
        self.aligned = self.rows % 16 == 0 and self.cols % 128 == 0
        self.order = net.order()

    def spot(self, owner):
        ox, oy = owner // self.net.gy, owner % self.net.gy
        down, beside = (oy, ox) if self.tall_axis == "gy" else (ox, oy)
        if isinstance(owner, int):
            return pl.ds(down * self.rows, self.rows), pl.ds(beside * self.cols, self.cols), beside
        row = pl.multiple_of(down * self.rows, self.rows)
        col = pl.multiple_of(beside * self.cols, self.cols)
        return pl.ds(row, self.rows), pl.ds(col, self.cols), beside

    def fetch(self, me, sources, target, sems):
        if not self.aligned:
            pltpu.make_async_copy(sources[0], target, sems.at[0]).start()
            return
        masks = iter(self.order)
        for source in sources:
            for place in range(source.shape[0]):
                rows, cols, beside = self.spot(me ^ next(masks))
                pltpu.make_async_copy(source.at[place], target.at[rows, cols], sems.at[beside]).start()

    def arrive(self, target, sems, beside):
        if not self.aligned:
            if beside == 0:
                pltpu.make_async_copy(target, target, sems.at[0]).wait()
            return
        part = target.at[:, pl.ds(beside * self.cols, self.cols)]
        pltpu.make_async_copy(part, part, sems.at[beside]).wait()

    def arrive_to(self, target, sems, done, col):
        while done < self.beside and done * self.cols < col:
            self.arrive(target, sems, done)
            done += 1
        return done

    def send(self, slots_ref, source, targets, sem, beside):
        if not self.aligned:
            if beside == self.beside - 1:
                pltpu.make_async_copy(source, targets[0], sem).start()
            return
        net = self.net
        half = net.size // 2
        for other in range(net.gy if self.tall_axis == "gy" else net.gx):
            owner = beside * net.gy + other if self.tall_axis == "gy" else other * net.gy + beside
            rows, cols, _ = self.spot(owner)
            slot = slots_ref[owner]

            @pl.when(slot < half)
            def _():
                pltpu.make_async_copy(source.at[rows, cols], targets[0].at[slot], sem).start()

            @pl.when(slot >= half)
            def _():
                pltpu.make_async_copy(source.at[rows, cols], targets[1].at[slot - half], sem).start()

    def send_to(self, slots_ref, source, targets, sem, done, col):
        while done < self.beside and (done + 1) * self.cols <= col:
            self.send(slots_ref, source, targets, sem, done)
            done += 1
        return done


def call(body, outs, ins, scratch, out_specs=None, limit=LIMIT):
    return pl.pallas_call(
        body,
        out_shape=outs,
        name=body.func.__name__,
        in_specs=ins,
        out_specs=[VM] * len(outs) if out_specs is None else out_specs,
        scratch_shapes=scratch,
        compiler_params=pltpu.CompilerParams(vmem_limit_bytes=limit * MIB),
        cost_estimate=COST,
    )


def begin(source, target, sem):
    pltpu.make_async_copy(source, target, sem).start()


def end(target, sem):
    pltpu.make_async_copy(target, target, sem).wait()


def moments(received, number):
    total = jnp.sum(received, axis=0)
    mean = total[0:1] / number
    inverse = lax.rsqrt(total[1:2] / number - mean * mean + 1e-05)
    return mean, inverse


def copies_of(value, out_ref):
    def one(place, carry):
        out_ref[place] = value
        return carry

    lax.fori_loop(0, out_ref.shape[0], one, 0)


def typical(gs):
    reach = 1.7320508 * gs[0:1]
    total = 0.0
    for node, share in ((gs[1:2] - reach, 1 / 6), (gs[1:2], 2 / 3), (gs[1:2] + reach, 1 / 6)):
        total = total + share * node * sigmoid(node)
    return total


def pieces_of(row):
    first = row.astype(BF).astype(F32)
    second = (row - first).astype(BF).astype(F32)
    third = row - first - second
    return jnp.concatenate([first, second, third, jnp.zeros((13, row.shape[1]), F32)], axis=0).astype(BF)


def outer(left, right):
    return dot(jnp.broadcast_to(left.astype(BF), (16, left.shape[1])), pieces_of(right), TN)


def local_sum(rows_here, mine, sums, mean, inverse, gain, shift_part, gain_part):
    hats = (sums - rows_here * mean) * inverse
    return gain * inverse * (mine - rows_here * shift_part - gain_part * hats)


def norm_back(up, hat, live, gain, inverse, shift_part, gain_part):
    return gain * inverse * (up - live * (shift_part + hat * gain_part))


def row_id(rows):
    return lax.broadcasted_iota(jnp.int32, (rows, 1), 0)


def column_sums(total_ref, lanes, keep, chunk, base=None):
    first, second = 0.0, 0.0
    for at in range(0, total_ref.shape[0], chunk):
        value = total_ref[at : at + chunk, lanes]
        if base is not None:
            value = value - base
        kept = value * keep[at : at + chunk]
        first = first + jnp.sum(kept, axis=0, keepdims=True)
        second = second + jnp.sum(kept * value, axis=0, keepdims=True)
    return first, second


def in_body(g, blocks, count, info_ref, x_ref, small_ref, *refs):
    sources = refs[:count]
    h_ref, out_ref, w_ref, st_ref, wsem = refs[count:]
    blocks.fetch(info_ref[1], sources, w_ref, wsem)
    keep = (row_id(g.rows) < info_ref[0] * g.flat).astype(F32)
    step = 256
    blocks.arrive_to(w_ref, wsem, 0, g.features)
    for at in range(0, g.channels, step):
        lanes = slice(at, at + step)
        h_ref[:, lanes] = dot(x_ref[...], w_ref[lanes, :], NT)
        st_ref[0:1, lanes], st_ref[1:2, lanes] = column_sums(h_ref, lanes, keep, g.chunk)
    st_ref[2:3] = small_ref[...]
    copies_of(st_ref[...], out_ref)


def flat_rows(g, source, line, lanes):
    return jnp.concatenate(
        [source[pl.ds(view * g.flat + SIDE * line, SIDE + 1), lanes] for view in range(g.slots)], axis=0
    )


def to_flat(g, band, target, line, lanes):
    for view in range(g.slots):
        target[pl.ds(view * g.flat + SIDE * line, SIDE + 1), lanes] = band[view * (SIDE + 1) : (view + 1) * (SIDE + 1)]


def clear_padding(g, target):
    for view in range(g.slots):
        target[pl.ds(view * g.flat + g.pixels, SIDE), :] = jnp.zeros((SIDE, target.shape[1]), F32)


def band_mask(g):
    return (row_id(g.band) % (SIDE + 1)) < SIDE


def shift_rows(g, tall_ref, out_ref):
    for kx in range(3):
        for at in range(0, g.tall, g.band):
            start, stop = at + kx - 1, at + kx - 1 + g.band
            if start < 0 or stop > g.tall:
                rows = pltpu.roll(tall_ref[at : at + g.band], (1 - kx) % g.band, 0)
            else:
                rows = tall_ref[start:stop]
            out_ref[kx, at : at + g.band] = rows.astype(BF)


def mid_body(g, blocks, count, info_ref, h_ref, got_ref, gs_ref, *refs):
    sources = refs[:count]
    a_hbm, hat_ref, h2_ref, st_ref, out_ref, bn_ref, a_ref, w_ref, q_ref, wsem, osem = refs[count:]
    blocks.fetch(info_ref[1], sources, w_ref, wsem)
    c = g.channels
    total = jnp.sum(got_ref[...], axis=0)
    number = jnp.max(total[2:3, c - 1 : c]) * float(g.pixels)
    mean = total[0:1] / number
    inverse = lax.rsqrt(total[1:2] / number - mean * mean + 1e-05)
    bn_ref[0:1] = mean
    bn_ref[1:2] = inverse
    bn_ref[2:3] = jnp.full((1, c), number, F32)
    inside = band_mask(g)
    q_ref[0 : g.band] = jnp.zeros((g.band, c), F32)
    q_ref[g.tall - g.band : g.tall] = jnp.zeros((g.band, c), F32)
    step = 256
    for line in range(SIDE):
        at = line * g.band
        for lane in range(0, c, step):
            lanes = slice(lane, lane + step)
            hat = (flat_rows(g, h_ref, line, lanes) - mean[:, lanes]) * inverse[:, lanes]
            hat_ref[at : at + g.band, lanes] = hat.astype(BF)
            n = hat * gs_ref[0:1, lanes] + gs_ref[1:2, lanes]
            q_ref[g.band + at : 2 * g.band + at, lanes] = jnp.where(inside, n * sigmoid(n), 0.0)
    shift_rows(g, q_ref, a_ref)
    begin(a_ref, a_hbm, osem)
    row = row_id(g.rows)
    live = ((row % (SIDE + 1)) < SIDE) & ((row % g.band) < info_ref[0] * (SIDE + 1))
    keep = live.astype(F32)
    done = 0
    for at in range(0, c, step):
        h2 = None
        for ky in range(3):
            for kx in range(3):
                tap = 3 * ky + kx
                done = blocks.arrive_to(w_ref, wsem, done, c * 9)
                part = dot(
                    a_ref[kx, ky * g.band : ky * g.band + g.rows],
                    w_ref[at : at + step, tap * c : (tap + 1) * c],
                    NT,
                )
                h2 = part if h2 is None else h2 + part
        lanes = slice(at, at + step)
        h2_ref[:, lanes] = h2
        st_ref[0:1, lanes], st_ref[1:2, lanes] = column_sums(h2_ref, lanes, keep, g.band)
    copies_of(st_ref[...], out_ref)
    end(a_ref, osem)


def out_body(g, blocks, count, info_ref, h2_ref, got_ref, bn1_ref, gs_ref, *refs):
    sources = refs[:count]
    a2_ref, h3_hbm, st_ref, out_ref, bn_ref, hat_ref, w_ref, p_ref, t_ref, h3_ref, mo_ref, wsem, osem = refs[count:]
    blocks.fetch(info_ref[1], sources, w_ref, wsem)
    mean, inverse = moments(got_ref[...], bn1_ref[2:3])
    bn_ref[0:1] = mean
    bn_ref[1:2] = inverse
    inside = band_mask(g)
    c = g.channels
    step = 256
    clear_padding(g, p_ref)
    for line in range(SIDE):
        at = line * g.band
        for lane in range(0, c, step):
            lanes = slice(lane, lane + step)
            hat = (h2_ref[at : at + g.band, lanes] - mean[:, lanes]) * inverse[:, lanes]
            hat_ref[at : at + g.band, lanes] = hat.astype(BF)
            n = hat * gs_ref[0:1, lanes] + gs_ref[1:2, lanes]
            to_flat(g, jnp.where(inside, n * sigmoid(n), 0.0), p_ref, line, lanes)
    p_ref[g.pixels : g.pixels + 1] = typical(gs_ref[...])
    for at in range(0, g.rows, g.chunk):
        a2_ref[at : at + g.chunk] = p_ref[at : at + g.chunk].astype(BF)
    row = row_id(g.rows)
    keep = (((row % g.flat) < g.pixels) & (row < info_ref[0] * g.flat)).astype(F32)
    here = (info_ref[0] * g.pixels).astype(F32)
    done = 0
    for at in range(0, g.features, step):
        lanes = slice(at, at + step)
        done = blocks.arrive_to(w_ref, wsem, done, at + step)
        t_ref[...] = dot(a2_ref[...], w_ref[:, lanes], NN)
        base = t_ref[g.pixels : g.pixels + 1]
        for top in range(0, g.rows, g.chunk):
            h3_ref[top : top + g.chunk, lanes] = (t_ref[top : top + g.chunk] - base).astype(BF)
        begin(h3_ref.at[:, pl.ds(at, step)], h3_hbm.at[:, pl.ds(at, step)], osem)
        total, square = column_sums(t_ref, slice(0, step), keep, g.chunk, base)
        st_ref[0:1, lanes] = total
        mo_ref[0:1, lanes] = total / here
        mo_ref[1:2, lanes] = square - total * total / here
    copies_of(mo_ref[...].astype(BF), out_ref)
    end(h3_ref, osem)


def pool_body(
    g, h3_hbm, x_hbm, got_ref, counts_ref, bn1_ref, gs_ref, z_ref, pool_ref, fac_ref, s_ref, t_ref, bn_ref, slope_hbm, hat_hbm,
    h3_ref, x_ref, slope_ref, hat_ref, insem, osem,
):
    for chunk in range(g.chunks):
        rows = pl.ds(chunk * g.chunk, g.chunk)
        begin(h3_hbm.at[rows], h3_ref.at[rows], insem.at[chunk, 0])
        begin(x_hbm.at[rows], x_ref.at[rows], insem.at[chunk, 1])
    number = bn1_ref[2:3, 0:1]
    rows_of = counts_ref[...] * float(g.pixels)
    means = got_ref[:, 0, :].astype(F32)
    mean = jnp.sum(rows_of * means, axis=0, keepdims=True) / number
    apart = means - mean
    square = got_ref[:, 1, :].astype(F32) + rows_of * apart * apart
    bn_ref[0:1] = mean
    bn_ref[1:2] = lax.rsqrt(jnp.sum(square, axis=0, keepdims=True) / number + 1e-05)
    step = 256

    def one(chunk, carry):
        rows = pl.ds(pl.multiple_of(chunk * g.chunk, 16), g.chunk)
        end(h3_ref.at[rows], insem.at[chunk, 0])
        end(x_ref.at[rows], insem.at[chunk, 1])
        for at in range(0, g.features, step):
            lanes = slice(at, at + step)
            hat = (h3_ref[rows, lanes].astype(F32) - bn_ref[0:1, lanes]) * bn_ref[1:2, lanes]
            pre = hat * gs_ref[0:1, lanes] + gs_ref[1:2, lanes] + x_ref[rows, lanes].astype(F32)
            sigma = sigmoid(pre)
            out = pre * sigma
            slope = sigma + out * (1.0 - sigma)
            hat_ref[rows, lanes] = hat.astype(BF)
            slope_ref[rows, lanes] = slope.astype(BF)
            for table, value in ((pool_ref, out), (s_ref, slope), (t_ref, slope * hat)):
                for one_of in range(2):
                    first = one_of * g.flat
                    last = first + g.pixels - 1
                    part = jnp.sum(value[first:last], axis=0, keepdims=True) + value[last : last + 1]
                    table[pl.ds(2 * chunk + one_of, 1), lanes] = part
        begin(slope_ref.at[rows], slope_hbm.at[rows], osem.at[0])
        begin(hat_ref.at[rows], hat_hbm.at[rows], osem.at[1])
        return carry

    lax.fori_loop(0, g.chunks, one, 0)
    pooled = pool_ref[...] * (1.0 / g.pixels)
    pool_ref[...] = pooled
    factor = lax.rsqrt(jnp.mean(pooled * pooled, axis=1, keepdims=True) + 1e-06)
    fac_ref[...] = jnp.broadcast_to(factor, fac_ref.shape)
    z_ref[...] = (pooled * factor).astype(BF)
    end(slope_ref, osem.at[0])
    end(hat_ref, osem.at[1])


def pair_back_body(g, grad_ref, pool_ref, fac_ref, s_ref, t_ref, dp_ref, st_ref, out_ref):
    grad = grad_ref[...]
    pooled = pool_ref[...]
    factor = fac_ref[:, 0:1]
    along = jnp.sum(pooled * grad, axis=1, keepdims=True) * (1.0 / g.features)
    down = (factor * grad - pooled * (factor * factor * factor) * along) * (1.0 / g.pixels)
    dp_ref[...] = down
    st_ref[0:1] = jnp.sum(down * s_ref[...], axis=0, keepdims=True)
    st_ref[1:2] = jnp.sum(down * t_ref[...], axis=0, keepdims=True)
    copies_of(st_ref[...].astype(out_ref.dtype), out_ref)


def out_back_body(
    g, blocks, count, info_ref, slope_hbm, hat_hbm, dp_ref, got_ref, mine_ref, sums_ref, objective_ref, bn1_ref, bn3_ref, gs3_ref,
    hat2_hbm, gs2_ref, *refs,
):
    sources = refs[:count]
    dh3_hbm, dn2_ref, st_ref, out_ref, tot_ref, local_ref = refs[count : count + 6]
    slope_ref, hat_ref, dh3_ref, hat2_ref, w_ref, p_ref, c_ref, insem, hsem, wsem, osem = refs[count + 6 :]
    for chunk in range(g.chunks):
        rows = pl.ds(chunk * g.chunk, g.chunk)
        begin(slope_hbm.at[rows], slope_ref.at[rows], insem.at[chunk, 0])
        begin(hat_hbm.at[rows], hat_ref.at[rows], insem.at[chunk, 1])
    blocks.fetch(info_ref[1], sources, w_ref, wsem)
    begin(hat2_hbm, hat2_ref, hsem)
    number = bn1_ref[2:3, 0:1]
    total = jnp.sum(got_ref[...].astype(F32), axis=0)
    tot_ref[...] = total
    c_ref[0:2] = total / number
    c_ref[2:3] = gs3_ref[0:1] * bn3_ref[1:2]
    here = (info_ref[0] * g.pixels).astype(F32)
    local_ref[...] = local_sum(
        here, mine_ref[0:1], sums_ref[0:1], bn3_ref[0:1], bn3_ref[1:2], gs3_ref[0:1], c_ref[0:1], c_ref[1:2]
    )
    row = row_id(g.flat)
    step = 512

    def one(chunk, carry):
        rows = pl.ds(pl.multiple_of(chunk * g.chunk, 16), g.chunk)
        end(slope_ref.at[rows], insem.at[chunk, 0])
        end(hat_ref.at[rows], insem.at[chunk, 1])
        for at in range(0, g.features, step):
            lanes = slice(at, at + step)
            slope, hat = slope_ref[rows, lanes].astype(F32), hat_ref[rows, lanes].astype(F32)
            parts = []
            for one_of in range(2):
                view = 2 * chunk + one_of
                span = slice(one_of * g.flat, (one_of + 1) * g.flat)
                live = ((row < g.pixels) & (view < info_ref[0])).astype(F32)
                up = dp_ref[pl.ds(view, 1), lanes] * slope[span]
                parts.append(live * c_ref[2:3, lanes] * (up - (c_ref[0:1, lanes] + hat[span] * c_ref[1:2, lanes])))
            dh3_ref[rows, lanes] = jnp.concatenate(parts, axis=0).astype(BF)
        begin(dh3_ref.at[rows], dh3_hbm.at[rows], osem.at[0])
        return carry

    lax.fori_loop(0, g.chunks, one, 0)
    blocks.arrive_to(w_ref, wsem, 0, g.features)
    p_ref[...] = dot(dh3_ref[...], w_ref[...], NT)
    end(hat2_ref, hsem)
    inside = band_mask(g)
    step = 256
    for lane in range(0, g.channels, step):
        lanes = slice(lane, lane + step)
        first, second = 0.0, 0.0
        for line in range(SIDE):
            at = line * g.band
            hat = hat2_ref[at : at + g.band, lanes].astype(F32)
            n = hat * gs2_ref[0:1, lanes] + gs2_ref[1:2, lanes]
            up = jnp.where(inside, flat_rows(g, p_ref, line, lanes) * slope_of(n, sigmoid(n)), 0.0)
            dn2_ref[at : at + g.band, lanes] = up.astype(BF)
            first = first + jnp.sum(up, axis=0, keepdims=True)
            second = second + jnp.sum(up * hat, axis=0, keepdims=True)
        st_ref[0:1, lanes] = first
        st_ref[1:2, lanes] = second
    st_ref[2:3] = objective_ref[...]
    copies_of(st_ref[...], out_ref)
    end(dh3_ref, osem.at[0])


def out_grad_body(g, blocks, slots_ref, a2_hbm, dh3_hbm, gs2_ref, local_ref, *refs):
    targets, (a2_ref, dh3_ref, w_ref, insem, dsem, osem) = refs[:-6], refs[-6:]
    begin(a2_hbm, a2_ref, insem)
    step = 512
    for place, at in enumerate(range(0, g.features, step)):
        begin(dh3_hbm.at[:, pl.ds(at, step)], dh3_ref.at[:, pl.ds(at, step)], dsem.at[place])
    base = typical(gs2_ref[...])
    end(a2_ref, insem)
    done = 0
    for place, at in enumerate(range(0, g.features, step)):
        lanes = slice(at, at + step)
        end(dh3_ref.at[:, pl.ds(at, step)], dsem.at[place])
        grad = dot(a2_ref[...], dh3_ref[:, lanes], TN) - outer(base, local_ref[:, lanes])
        w_ref[:, lanes] = grad.astype(BF)
        done = blocks.send_to(slots_ref, w_ref, targets, osem, done, at + step)
    end(w_ref, osem)


def mid_back_body(
    g, blocks, count, info_ref, dn2_ref, got_ref, mine_ref, sums_ref, bn1_ref, bn2_ref, gs2_ref, hat2_ref, hat1_ref, gs1_ref, *refs,
):
    sources = refs[:count]
    dh2_ref, dn1_ref, out_ref, tot_ref, local_ref, w_ref, q_ref, d_ref, t_ref, st_ref, wsem = refs[count:]
    blocks.fetch(info_ref[1], sources, w_ref, wsem)
    number = bn1_ref[2:3, 0:1]
    total = jnp.sum(got_ref[...], axis=0)
    tot_ref[...] = total
    shift_part, gain_part = total[0:1] / number, total[1:2] / number
    here = (info_ref[0] * g.pixels).astype(F32)
    local_ref[...] = local_sum(
        here, mine_ref[0:1], sums_ref[0:1], bn2_ref[0:1], bn2_ref[1:2], gs2_ref[0:1], shift_part, gain_part
    )
    c = g.channels
    inside = band_mask(g)
    live = (inside & (row_id(g.band) < info_ref[0] * (SIDE + 1))).astype(F32)
    q_ref[0 : g.band] = jnp.zeros((g.band, c), F32)
    q_ref[g.tall - g.band : g.tall] = jnp.zeros((g.band, c), F32)
    step = 256
    for line in range(SIDE):
        at = line * g.band
        for lane in range(0, c, step):
            lanes = slice(lane, lane + step)
            hat = hat2_ref[at : at + g.band, lanes].astype(F32)
            down = norm_back(
                dn2_ref[at : at + g.band, lanes].astype(F32),
                hat,
                live,
                gs2_ref[0:1, lanes],
                bn2_ref[1:2, lanes],
                shift_part[:, lanes],
                gain_part[:, lanes],
            )
            dh2_ref[at : at + g.band, lanes] = down.astype(BF)
            q_ref[g.band + at : 2 * g.band + at, lanes] = down
    shift_rows(g, q_ref, d_ref)
    blocks.arrive_to(w_ref, wsem, 0, 9 * c)
    for lane in range(0, c, step):
        lanes = slice(lane, lane + step)
        da1 = None
        for ky in range(3):
            for kx in range(3):
                tap = 3 * ky + kx
                part = dot(
                    d_ref[2 - kx, (2 - ky) * g.band : (2 - ky) * g.band + g.rows],
                    w_ref[:, tap * c + lane : tap * c + lane + step],
                    NN,
                )
                da1 = part if da1 is None else da1 + part
        t_ref[...] = da1
        first, second = 0.0, 0.0
        for line in range(SIDE):
            at = line * g.band
            hat = hat1_ref[at : at + g.band, lanes].astype(F32)
            n = hat * gs1_ref[0:1, lanes] + gs1_ref[1:2, lanes]
            up = jnp.where(inside, t_ref[at : at + g.band] * slope_of(n, sigmoid(n)), 0.0)
            dn1_ref[at : at + g.band, lanes] = up.astype(BF)
            first = first + jnp.sum(up, axis=0, keepdims=True)
            second = second + jnp.sum(up * hat, axis=0, keepdims=True)
        st_ref[0:1, lanes] = first
        st_ref[1:2, lanes] = second
    copies_of(st_ref[...], out_ref)


def mid_grad_body(g, blocks, slots_ref, dh2_hbm, a_hbm, gs1_ref, local_ref, *refs):
    targets, (dh2_ref, a_ref, w_ref, base_ref, insem, asem, osem) = refs[:-7], refs[-7:]
    begin(dh2_hbm, dh2_ref, insem)
    for kx in range(3):
        begin(a_hbm.at[kx], a_ref.at[kx], asem.at[kx])
    c = g.channels
    shared = jnp.broadcast_to(typical(gs1_ref[...]).astype(BF), (16, c))
    base_ref[...] = dot(pieces_of(local_ref[...]), shared, TN)
    end(dh2_ref, insem)
    done = 0
    for ky in range(3):
        for kx in range(3):
            tap = 3 * ky + kx
            if ky == 0:
                end(a_ref.at[kx], asem.at[kx])
            part = dot(dh2_ref[...], a_ref[kx, ky * g.band : ky * g.band + g.rows], TN)
            w_ref[:, tap * c : (tap + 1) * c] = (part - base_ref[...]).astype(BF)
            done = blocks.send_to(slots_ref, w_ref, targets, osem, done, (tap + 1) * c)
    end(w_ref, osem)


def in_back_body(g, info_ref, dn1_ref, got_ref, bn1_ref, gs1_ref, hat1_ref, dh1_ref, tot_ref, p_ref):
    number = bn1_ref[2:3, 0:1]
    total = jnp.sum(got_ref[...], axis=0)
    tot_ref[...] = total
    shift_part, gain_part = total[0:1] / number, total[1:2] / number
    live = (band_mask(g) & (row_id(g.band) < info_ref[0] * (SIDE + 1))).astype(F32)
    clear_padding(g, p_ref)
    step = 256
    for line in range(SIDE):
        at = line * g.band
        for lane in range(0, g.channels, step):
            lanes = slice(lane, lane + step)
            down = norm_back(
                dn1_ref[at : at + g.band, lanes].astype(F32),
                hat1_ref[at : at + g.band, lanes].astype(F32),
                live,
                gs1_ref[0:1, lanes],
                bn1_ref[1:2, lanes],
                shift_part[:, lanes],
                gain_part[:, lanes],
            )
            to_flat(g, down, p_ref, line, lanes)
    for at in range(0, g.rows, g.chunk):
        dh1_ref[at : at + g.chunk] = p_ref[at : at + g.chunk].astype(BF)


def in_grad_body(g, blocks, slots_ref, dh1_ref, x_hbm, *refs):
    targets, (x_ref, w_ref, xsem, gsem) = refs[:-4], refs[-4:]
    step = 512
    for place, at in enumerate(range(0, g.features, step)):
        begin(x_hbm.at[:, pl.ds(at, step)], x_ref.at[:, pl.ds(at, step)], xsem.at[place])
    done = 0
    for place, at in enumerate(range(0, g.features, step)):
        lanes = slice(at, at + step)
        end(x_ref.at[:, pl.ds(at, step)], xsem.at[place])
        w_ref[:, lanes] = dot(dh1_ref[...], x_ref[:, lanes], TN).astype(BF)
        done = blocks.send_to(slots_ref, w_ref, targets, gsem, done, at + step)
    end(w_ref, gsem)


def views_grad_body(g, blocks, count, info_ref, dh1_ref, slope_ref, dp_ref, *refs):
    sources = refs[:count]
    out_ref, w_ref, wsem = refs[count:]
    step = out_ref.shape[2]
    turn = pl.program_id(0)

    @pl.when(turn == 0)
    def _():
        blocks.fetch(info_ref[1], sources, w_ref, wsem)

    for one_of in range(g.features // step):

        @pl.when(turn == one_of)
        def _():
            done = -(-one_of * step // blocks.cols) if blocks.aligned else one_of
            blocks.arrive_to(w_ref, wsem, done, (one_of + 1) * step)

    lanes = pl.ds(pl.multiple_of(turn * step, step), step)
    total = dot(dh1_ref[...], w_ref[:, lanes], NN)
    slope = slope_ref[...].astype(F32)
    for view in range(g.slots):
        rows = slice(view * g.flat, view * g.flat + g.pixels)
        out_ref[view] = total[rows] + dp_ref[view : view + 1] * slope[rows]


def norm_grad_body(share, info_ref, first_ref, second_ref, third_ref, out_ref, all_ref):
    at = 0
    for part_ref in (first_ref, second_ref, third_ref):
        for row in (1, 0):
            all_ref[:, at : at + part_ref.shape[1]] = part_ref[row : row + 1]
            at += part_ref.shape[1]
    turn = lax.rem(all_ref.shape[1] - info_ref[1] * share, all_ref.shape[1])
    out_ref[...] = pltpu.roll(all_ref[...], turn, 1)[:, :share]


def per_device(views, counts, partners, w_in, w_mid, w_out, norm_params):
    slot_count, pixels, features = views.shape
    pair_count = partners.shape[1]
    net = Net(lax.axis_size("gx"), lax.axis_size("gy"))
    size = net.size
    channels = w_in.shape[1] * net.gy
    g = Grid(slot_count, features, channels)
    me = lax.axis_index("gx") * net.gy + lax.axis_index("gy")
    order = net.order()
    place = [order.index(mask) for mask in range(size)]
    slots = jnp.asarray(place, jnp.int32)[me ^ jnp.arange(size, dtype=jnp.int32)]
    sources = me ^ jnp.asarray(order, jnp.int32)
    info = jnp.stack([counts[0], me.astype(jnp.int32)])

    shards = {"in": w_in.T, "mid": w_mid.T, "out": w_out}
    blocks = {
        name: Blocks(net, shard.shape, "gx" if name == "out" else "gy") for name, shard in shards.items()
    }

    def pick(places, table):
        chooser = (places[:, None] == jnp.arange(size, dtype=jnp.int32)[None, :]).astype(BF)
        return jnp.dot(chooser, table.reshape(size, -1), preferred_element_type=F32).astype(BF).reshape(table.shape)

    def whole(name, held):
        pieces = net.gather_core(held)
        plan = blocks[name]
        if plan.aligned:
            return pieces
        table = pick(slots, jnp.concatenate(pieces)).reshape((net.gx, net.gy) + plan.shape)
        return [table.transpose((1, 2, 0, 3) if plan.tall_axis == "gy" else (0, 2, 1, 3)).reshape(plan.whole)]

    def grad_shapes(name):
        plan = blocks[name]
        if plan.aligned:
            return [jax.ShapeDtypeStruct((size // 2,) + plan.shape, BF)] * 2
        return [jax.ShapeDtypeStruct(plan.whole, BF)]

    def reduce_core(name, grads, *done):
        plan = blocks[name]
        if not plan.aligned:
            rows, cols = plan.shape
            if plan.tall_axis == "gy":
                table = grads[0].reshape(net.gy, rows, net.gx, cols).transpose(2, 0, 1, 3)
            else:
                table = grads[0].reshape(net.gx, rows, net.gy, cols).transpose(0, 2, 1, 3)
            table = pick(sources, table.reshape(size, rows, cols))
            grads = [table[: size // 2], table[size // 2 :]]
        return net.reduce_core(*grads, *done)

    sem = pltpu.SemaphoreType.DMA
    f32 = lambda *shape: jax.ShapeDtypeStruct(shape, F32)
    b16 = lambda *shape: jax.ShapeDtypeStruct(shape, BF)
    v32 = lambda *shape: pltpu.VMEM(shape, F32)
    v16 = lambda *shape: pltpu.VMEM(shape, BF)
    weight = lambda name: pltpu.VMEM(blocks[name].whole, BF)
    arrivals = lambda name: sem((blocks[name].beside,))

    held_in = net.gather_far(shards["in"])
    x = jnp.pad(views, ((0, 0), (0, g.flat - pixels), (0, 0))).reshape(g.rows, features)
    held_mid = net.gather_far(tie(shards["mid"], held_in))
    held_in |= net.gather_near(held_in)
    held_in = tie(held_in, x, slots, info)
    held_out = net.gather_far(tie(shards["out"], held_mid))
    held_in |= net.gather_last(held_in)
    held_mid |= net.gather_near(tie(held_mid, held_in))
    held_out = tie(held_out, held_in)
    full_in = whole("in", held_in)
    share = norm_params.shape[0]
    listed = slot_count * pair_count
    small = jnp.concatenate(
        [
            norm_params.astype(F32),
            partners.reshape(-1).astype(F32),
            jnp.zeros((channels - 1 - share - listed,), F32),
            counts.astype(F32),
        ]
    )[None]

    pieces = len(full_in)
    h1, copies = call(
        functools.partial(in_body, g, blocks["in"], pieces),
        [f32(g.rows, channels), f32(size, 3, channels)],
        [SM, VM, VM] + [HBM] * pieces,
        [weight("in"), v32(3, channels), arrivals("in")],
        limit=24,
    )(info, x, small, *full_in)
    got = net.spread(copies)
    held_mid |= net.gather_last(tie(held_mid, h1))
    full_mid = whole("mid", held_mid)

    norm_values = got[:, 2, :share].reshape(-1)
    gs1 = norm_values[0 : 2 * channels].reshape(2, channels)
    gs2 = norm_values[2 * channels : 4 * channels].reshape(2, channels)
    gs3 = norm_values[4 * channels :].reshape(2, features)

    held_out |= net.gather_near(tie(held_out, held_mid, gs1))
    pieces = len(full_mid)
    a1, hat1, h2, sums2, copies, bn1 = call(
        functools.partial(mid_body, g, blocks["mid"], pieces),
        [
            b16(3, g.tall, channels),
            b16(g.rows, channels),
            f32(g.rows, channels),
            f32(2, channels),
            f32(size, 2, channels),
            f32(3, channels),
        ],
        [SM, VM, VM, VM] + [HBM] * pieces,
        [v16(3, g.tall, channels), weight("mid"), v32(g.tall, channels), arrivals("mid"), sem(())],
        out_specs=[HBM, VM, VM, VM, VM, VM],
    )(info, h1, got, gs1, *full_mid)
    targets = got[:, 2, share : share + listed].reshape(size * slot_count, pair_count).astype(jnp.int32)
    occupied = got[:, 2, channels - 1]
    got = net.spread(copies)
    held_out = tie(held_out, h2)
    held_out |= net.gather_last(held_out)
    full_out = whole("out", held_out)

    pieces = len(full_out)
    a2, h3, sums3, copies, bn2, hat2 = call(
        functools.partial(out_body, g, blocks["out"], pieces),
        [
            b16(g.rows, channels),
            b16(g.rows, features),
            f32(1, features),
            b16(size, 2, features),
            f32(2, channels),
            b16(g.rows, channels),
        ],
        [SM, VM, VM, VM, VM] + [HBM] * pieces,
        [
            weight("out"),
            v32(g.rows, channels),
            v32(g.rows, 256),
            v16(g.rows, features),
            v32(2, features),
            arrivals("out"),
            sem(()),
        ],
        out_specs=[VM, HBM, VM, VM, VM, VM],
    )(info, h2, got, bn1, gs2, *full_out)

    got = net.spread(copies)
    view_ids = jnp.arange(size * slot_count, dtype=jnp.int32)
    filled = ((view_ids % slot_count).astype(F32) < jnp.repeat(occupied, slot_count)).astype(F32)
    chosen = [(targets[:, k : k + 1] == view_ids[None, :]).astype(F32) * filled[:, None] for k in range(pair_count)]
    pairs = sum(chosen)
    links = pairs + pairs.T
    degree = jnp.sum(links, axis=1, keepdims=True)
    per_view = f32(slot_count, features)
    z, pooled, factor, slope_sum, slope_hat, bn3, slope, hat = call(
        functools.partial(pool_body, g),
        [b16(slot_count, features), per_view, f32(slot_count, 128), per_view, per_view, f32(2, features)]
        + [b16(g.rows, features)] * 2,
        [HBM, HBM] + [VM] * 4,
        [
            v16(g.rows, features),
            v16(g.rows, features),
            v16(g.rows, features),
            v16(g.rows, features),
            sem((g.chunks, 2)),
            sem((2,)),
        ],
        out_specs=[VM] * 6 + [HBM] * 2,
    )(h3, x, got, occupied[:, None], bn1, gs3)

    width = features // size
    embeds = lax.all_to_all(z.reshape(slot_count, size, width).transpose(1, 0, 2), AX, 0, 0, tiled=True)
    embeds = embeds.reshape(size * slot_count, width)
    embeds_f = embeds.astype(F32)
    grad_embed = 2.0 * (degree * embeds_f - jnp.dot(links.astype(BF), embeds, preferred_element_type=F32))
    objective = 0.0
    for one in chosen:
        gap = filled[:, None] * embeds_f - jnp.dot(one.astype(BF), embeds, preferred_element_type=F32)
        objective = objective + jnp.sum(gap * gap)
    objective = jnp.full((1, channels), objective, F32)
    grad_embed = lax.all_to_all(grad_embed.reshape(size, slot_count, width), AX, 0, 0, tiled=True)
    grad_embed = grad_embed.transpose(1, 0, 2).reshape(slot_count, features)

    grad_pooled, mine3, copies = call(
        functools.partial(pair_back_body, g),
        [per_view, f32(2, features), b16(size, 2, features)],
        [VM] * 5,
        [],
    )(grad_embed, pooled, factor, slope_sum, slope_hat)
    got = net.spread(copies)
    pieces = len(full_out)
    dh3, dn2, mine2, copies, total3, local3 = call(
        functools.partial(out_back_body, g, blocks["out"], pieces),
        [
            b16(g.rows, features),
            b16(g.rows, channels),
            f32(3, channels),
            f32(size, 3, channels),
            f32(2, features),
            f32(1, features),
        ],
        [SM, HBM, HBM] + [VM] * 8 + [HBM, VM] + [HBM] * pieces,
        [
            v16(g.rows, features),
            v16(g.rows, features),
            v16(g.rows, features),
            v16(g.rows, channels),
            weight("out"),
            v32(g.rows, channels),
            v32(3, features),
            sem((g.chunks, 2)),
            sem(()),
            arrivals("out"),
            sem((2,)),
        ],
        out_specs=[HBM, VM, VM, VM, VM, VM],
    )(info, slope, hat, grad_pooled, got, mine3, sums3, objective, bn1, bn3, gs3, hat2, gs2, *full_out)

    got = net.spread(copies)
    grads = call(
        functools.partial(out_grad_body, g, blocks["out"]),
        grad_shapes("out"),
        [SM, HBM, HBM, VM, VM],
        [v16(g.rows, channels), v16(g.rows, features), weight("out"), sem(()), sem((features // 512,)), sem(())],
        out_specs=[HBM] * len(grad_shapes("out")),
    )(slots, a2, dh3, gs2, local3)
    sum_out = reduce_core("out", grads)

    pieces = len(full_mid)
    dh2, dn1, copies, total2, local2 = call(
        functools.partial(mid_back_body, g, blocks["mid"], pieces),
        [b16(g.rows, channels), b16(g.rows, channels), f32(size, 2, channels), f32(3, channels), f32(1, channels)],
        [SM] + [VM] * 10 + [HBM] * pieces,
        [
            weight("mid"),
            v32(g.tall, channels),
            v16(3, g.tall, channels),
            v32(g.rows, 256),
            v32(2, channels),
            arrivals("mid"),
        ],
    )(info, dn2, tie(got, *grads), mine2, sums2, bn1, bn2, gs2, hat2, hat1, gs1, *full_mid)
    got = net.spread(copies)
    grads = call(
        functools.partial(mid_grad_body, g, blocks["mid"]),
        grad_shapes("mid"),
        [SM, HBM, HBM, VM, VM],
        [
            v16(g.rows, channels),
            v16(3, g.tall, channels),
            weight("mid"),
            v32(channels, channels),
            sem(()),
            sem((3,)),
            sem(()),
        ],
        out_specs=[HBM] * len(grad_shapes("mid")),
    )(slots, dh2, a1, gs1, local2)
    sum_mid = reduce_core("mid", grads)

    dh1, total1 = call(
        functools.partial(in_back_body, g),
        [b16(g.rows, channels), f32(2, channels)],
        [SM] + [VM] * 5,
        [v32(g.rows, channels)],
    )(info, dn1, tie(got, *grads), bn1, gs1, hat1)
    grads = call(
        functools.partial(in_grad_body, g, blocks["in"]),
        grad_shapes("in"),
        [SM, VM, HBM],
        [v16(g.rows, features), weight("in"), sem((features // 512,)), sem(())],
        out_specs=[HBM] * len(grad_shapes("in")),
    )(slots, tie(dh1, sum_mid), x)
    sum_mid = net.reduce_last(sum_mid)
    sum_out = net.reduce_last(tie(sum_out, *grads))
    sum_in = reduce_core("in", grads, sum_mid)

    step = 512
    pieces = len(full_in)
    whole_rows = lambda cols: pl.BlockSpec((g.rows, cols), lambda i: (0, 0))
    views_grad = pl.pallas_call(
        functools.partial(views_grad_body, g, blocks["in"], pieces),
        grid=(features // step,),
        out_shape=f32(slot_count, pixels, features),
        in_specs=[
            SM,
            whole_rows(channels),
            pl.BlockSpec((g.rows, step), lambda i: (0, i)),
            pl.BlockSpec((slot_count, step), lambda i: (0, i)),
        ]
        + [HBM] * pieces,
        out_specs=pl.BlockSpec((slot_count, pixels, step), lambda i: (0, 0, i)),
        scratch_shapes=[weight("in"), arrivals("in")],
        compiler_params=pltpu.CompilerParams(vmem_limit_bytes=LIMIT * MIB),
        cost_estimate=COST,
        name="views_grad_body",
    )(info, tie(dh1, sum_in), slope, grad_pooled, *full_in)

    sum_in = net.reduce_last(sum_in)
    own_out = net.reduce_far(net.reduce_near(sum_out))
    sum_mid = tie(net.reduce_near(sum_mid), views_grad)
    sum_in = net.reduce_near(tie(sum_in, views_grad))
    own_mid = net.reduce_far(sum_mid).T
    own_in = net.reduce_far(sum_in).T

    loss_value = total2[2, 0] / (pair_count * features * jnp.sum(occupied))
    norm_grad = call(
        functools.partial(norm_grad_body, share),
        [f32(1, share)],
        [SM, VM, VM, VM],
        [v32(1, 4 * channels + 2 * features)],
    )(info, tie(total1, *grads), total2, total3)[0].reshape(share)
    return (loss_value, views_grad, own_in, own_mid, own_out, norm_grad)


def solution(mesh):
    weights = P("gx", "gy")
    in_specs = (P(AX, None, None), P(AX), P(AX, None), weights, weights, weights, P(AX))
    out_specs = (P(), P(AX, None, None), weights, weights, weights, P(AX))
    return jax.shard_map(
        per_device, mesh=mesh, in_specs=in_specs, out_specs=out_specs, check_vma=False
    )
```
